32 devices in a mesh: dp: 4 (over z), cent: 8 (over y, x, core).
Axes of the slice: x: 2, y: 2, z: 4, core: 2. Of those that a mesh axis runs over, the one named last changes fastest.
Arguments:
- points: bfloat16 [4096, 1024], P(('dp', 'cent')), may hold values from -6 to 6
- centroids: bfloat16 [32768, 1024], P('cent'), may hold values from -6 to 6
Outputs:
- centroids_next: float32 [1024, 32768], P('dp', 'cent')
The draws below stay inside these ranges and needn't reach their ends.
All inputs are finite; a program needn't handle non-finite values.
Results may differ from the reference program's by a relative error of at most 0.007.
Values may be sent and summed in bfloat16 or wider, within the bound.
A program may use at most 128 MiB of HBM per device.

```python
import jax
import jax.numpy as jnp
from jax import lax

D = 1024
K = 32768
ROWS = 4096
N_DP = 4


def centroid_rows(key, row_ids):
    base_key = jax.random.fold_in(key, 9137)

    def single_row(row_id):
        row_key = jax.random.fold_in(base_key, row_id)
        return jnp.clip(jax.random.normal(row_key, (D,), jnp.float32), -6.0, 6.0)
    return jax.vmap(single_row)(row_ids)


def draw_centroids(key, part):
    matrix = centroid_rows(key, jnp.arange(K, dtype=jnp.int32))
    return matrix.astype(jnp.bfloat16)


def draw_points(key, part):
    value_key = jax.random.fold_in(key, 4421)
    return jnp.clip(jax.random.normal(value_key, (ROWS, D), jnp.float32), -6.0, 6.0).astype(jnp.bfloat16)


def setup_inputs(seed: int = 0) -> dict:
    keys = jax.random.split(jax.random.key(seed), 3)
    points = draw_points(jax.random.fold_in(keys[2], 71), 0)
    centroids = draw_centroids(jax.random.fold_in(keys[2], 71), 0)
    return dict(points=points, centroids=centroids)


BETA_GAIN = 4.0
PRIOR = 0.5


def reference(points, centroids):
    sharpness = BETA_GAIN * D ** -0.5
    cent_vals = centroids.astype(jnp.float32)
    sqnorm = jnp.sum(cent_vals * cent_vals, axis=1)
    group_size = ROWS // N_DP
    block_rows = min(512, group_size)
    grouped = points.reshape(N_DP, group_size // block_rows, block_rows, D)

    def block_step(carry, xblock):
        counts_acc, numer_acc = carry
        point_vals = xblock.astype(jnp.float32)
        dots = jnp.dot(point_vals, cent_vals.T, precision=lax.Precision.HIGHEST)
        logits = sharpness * (dots - 0.5 * sqnorm[None, :])
        row_top = jnp.max(logits, axis=1, keepdims=True)
        weights = jnp.exp(logits - row_top)
        row_total = jnp.sum(weights, axis=1, keepdims=True)
        resp = lax.optimization_barrier((weights / row_total).astype(jnp.bfloat16)).astype(jnp.float32)
        counts_acc = counts_acc + jnp.sum(resp, axis=0)
        numer_acc = numer_acc + jnp.dot(resp.T, point_vals, precision=lax.Precision.HIGHEST)
        return (counts_acc, numer_acc), None

    def group_step(carry, blocks):
        counts_all, numer_all = carry
        begin = (jnp.zeros((K,), jnp.float32), jnp.zeros((K, D), jnp.float32))
        (counts_part, numer_part), _ = lax.scan(block_step, begin, blocks)
        numer_part = lax.optimization_barrier(numer_part.astype(jnp.bfloat16)).astype(jnp.float32)
        return (counts_all + counts_part, numer_all + numer_part), None

    begin_all = (jnp.zeros((K,), jnp.float32), jnp.zeros((K, D), jnp.float32))
    (counts, numer), _ = lax.scan(group_step, begin_all, grouped)
    updated = (numer + PRIOR * cent_vals) / (counts[:, None] + PRIOR)
    return updated.T
```

```python
import functools
import math

import jax
import jax.numpy as jnp
from jax import lax
from jax.experimental import pallas as pl
from jax.experimental.pallas import tpu as pltpu
from jax.sharding import PartitionSpec as P

BETA_GAIN = 4.0
PRIOR = 0.5
MESH = pl.DeviceIdType.MESH
NT = (((1,), (1,)), ((), ()))


def general(points, centroids):
    features = points.shape[1]
    sharpness = BETA_GAIN * features ** (-0.5)
    gathered = lax.all_gather(points, "cent", axis=0, tiled=True)
    sqnorm = jnp.sum(jnp.square(centroids.astype(jnp.float32)), axis=1)
    total_rows = gathered.shape[0]
    block_rows = min(512, total_rows)
    blocks = gathered.reshape(total_rows // block_rows, block_rows, features)
    shard_cents = centroids.shape[0]

    def logits_of(xblock):
        dots = lax.dot_general(xblock, centroids, NT, preferred_element_type=jnp.float32)
        return sharpness * (dots - 0.5 * sqnorm[None, :])

    def resp_of(logits, row_top, row_total):
        return (jnp.exp(logits - row_top[:, None]) / row_total[:, None]).astype(jnp.bfloat16)

    logits = lax.map(logits_of, blocks)
    local_max = jnp.max(logits, axis=-1)
    local_sum = jnp.sum(jnp.exp(logits - local_max[..., None]), axis=-1)
    row_top = lax.pmax(local_max, "cent")
    row_total = lax.psum(local_sum * jnp.exp(local_max - row_top), "cent")
    resp = jax.vmap(resp_of)(logits, row_top, row_total)
    resp = resp.reshape(total_rows, shard_cents)
    counts = jnp.sum(resp.astype(jnp.float32), axis=0)
    dp_count = lax.axis_size("dp")
    dp_index = lax.axis_index("dp")
    column_share = features // dp_count
    numer = lax.psum_scatter(
        lax.dot_general(
            gathered, resp, (((0,), (0,)), ((), ())), preferred_element_type=jnp.float32
        ).astype(jnp.bfloat16),
        "dp",
        scatter_dimension=0,
        tiled=True,
    ).astype(jnp.float32)
    counts_all = lax.psum(counts, "dp")
    own_cols = (
        lax.dynamic_slice_in_dim(centroids, dp_index * column_share, column_share, 1)
        .astype(jnp.float32)
        .T
    )
    return (numer + PRIOR * own_cols) / (counts_all[None, :] + PRIOR)


NZ = 4
NC = 8
CHUNK = 1024


def fused(
    points_ref, cents_ref, out_ref,
    x_ref, c_ref, e_ref, xt_ref, a_ref, bias_ref, buf0, buf1, obuf, mstat, scale_ref, gath,
    load_sem, send_sem, recv_sem, stat_send, stat_recv, out_sem,
):
    shard, feats = points_ref.shape
    kc = cents_ref.shape[0]
    n_chunk = kc // CHUNK
    block = 2 * shard
    group = NC * shard
    own_feats = feats // NZ
    gain = BETA_GAIN * feats ** (-0.5) * math.log2(math.e)

    z = lax.axis_index("dp")
    cent = lax.axis_index("cent")
    core = cent % 2
    xx = (cent // 2) % 2
    yy = cent // 4
    flip = z // 2
    zz = z + flip * (3 - 2 * z)

    def z_of(j):
        s = (1 - zz) if j == 1 else (zz if j == 0 else j)
        return s + flip * (3 - 2 * s)

    def pos_of(pos):
        fx = pos in ("x", "d")
        fy = pos in ("y", "d")
        return ((1 - yy) if fy else yy) * 2 + ((1 - xx) if fx else xx)

    x_peer = (z, (yy * 2 + 1 - xx) * 2 + core)
    y_peer = (z, ((1 - yy) * 2 + xx) * 2 + core)
    sib = (z, cent + 1 - 2 * core)

    def piece(sid):
        return x_ref.at[pl.ds(pl.multiple_of(sid * shard, shard), shard)]

    def sid_of(j, pos, other=False):
        return z_of(j) * NC + pos_of(pos) * 2 + ((1 - core) if other else core)

    def copy_to(sid, dev, slot):
        return pltpu.make_async_remote_copy(
            src_ref=piece(sid), dst_ref=piece(sid), send_sem=send_sem.at[slot],
            recv_sem=recv_sem.at[sid], device_id=dev, device_id_type=MESH,
        )

    def wait_piece(sid):
        copy_to(sid, sib, 0).wait_recv()

    POS = {"c": 0, "x": 1, "y": 2, "d": 3}

    def routes(j, pos):
        base = (j * 4 + POS[pos]) * 5
        r = []
        if pos == "c":
            zj = z_of(j)
            up = (zj <= z) & (z < NZ - 1)
            down = (zj >= z) & (z > 0)
            r.append((up, (z + 1, cent), base))
            r.append((down, (z - 1, cent), base + 1))
            r.append((None, x_peer, base + 2))
            r.append((None, y_peer, base + 3))
        if pos == "x" and j % 2 == 0:
            r.append((None, y_peer, base + 3))
        if pos == "y" and j % 2 == 1:
            r.append((None, x_peer, base + 2))
        r.append((None, sib, base + 4))
        return r

    def each_route(j, pos, act):
        sid = sid_of(j, pos)
        for cond, dev, slot in routes(j, pos):
            if cond is None:
                act(copy_to(sid, dev, slot))
            else:
                @pl.when(cond)
                def _(dev=dev, slot=slot):
                    act(copy_to(sid, dev, slot))

    def pass_on(j, pos):
        if (j, pos) != (0, "c"):
            wait_piece(sid_of(j, pos))
        each_route(j, pos, lambda c: c.start())

    own_id = sid_of(0, "c")
    load_x = pltpu.make_async_copy(points_ref, piece(own_id), load_sem.at[0])
    load_c = pltpu.make_async_copy(cents_ref, c_ref, load_sem.at[1])
    load_x.start()
    load_c.start()
    barrier = pltpu.get_barrier_semaphore()
    for d in range(1, NC):
        pl.semaphore_signal(barrier, inc=1, device_id=(z, (cent + d) % NC), device_id_type=MESH)

    @pl.when(z > 0)
    def _():
        pl.semaphore_signal(barrier, inc=1, device_id=(z - 1, cent), device_id_type=MESH)

    @pl.when(z < NZ - 1)
    def _():
        pl.semaphore_signal(barrier, inc=1, device_id=(z + 1, cent), device_id_type=MESH)

    inner_z = jnp.minimum(z, 1) * jnp.minimum(NZ - 1 - z, 1)
    pl.semaphore_wait(barrier, NC + inner_z)

    load_x.wait()
    pass_on(0, "c")
    load_c.wait()

    def norm_step(r, _):
        rows = pl.ds(pl.multiple_of(r * 256, 256), 256)
        v = c_ref[rows, :].astype(jnp.float32)
        s = jnp.sum(v * v, axis=1, keepdims=True) * (0.5 * gain)
        bias_ref[rows, :] = jnp.broadcast_to(s, (256, 128))
        return 0

    lax.fori_loop(0, kc // 256, norm_step, 0)

    def stat_copy(j, d):
        zj = z_of(j)
        return pltpu.make_async_remote_copy(
            src_ref=gath.at[cent, zj], dst_ref=gath.at[cent, zj],
            send_sem=stat_send.at[j, d], recv_sem=stat_recv.at[cent, zj],
            device_id=(z, (cent + d) % NC), device_id_type=MESH,
        )

    own_col = pl.ds(pl.multiple_of(z * own_feats, own_feats), own_feats)
    bufs = (buf0, buf1)

    def step(n, _):
        for at, items in (
            (1, ((0, "x"), (0, "y"), (1, "c"))),
            (4, ((0, "d"), (1, "x"), (1, "y"), (2, "c"))),
            (8, ((1, "d"), (2, "x"), (2, "y"), (3, "c"))),
            (12, ((2, "d"), (3, "x"), (3, "y"))),
            (15, ((3, "d"),)),
        ):
            @pl.when(n == at)
            def _(items=items):
                for j, pos in items:
                    pass_on(j, pos)

        g, r = n // 4, n % 4
        last = n // 15
        first = 1 - jnp.minimum(n, 1)
        r0 = 1 - jnp.minimum(r, 1)
        r3 = r // 3
        j = g - r0 + first + r3 - last
        fx = jnp.where(r == 1, 1, 0) + r0 - first + last
        fy = jnp.where(r == 2, 1, 0) + r0 - first + last
        j1 = jnp.where(j == 1, 1, 0)
        j0 = jnp.where(j == 0, 1, 0)
        s = j0 * zz + j1 * (1 - zz) + (1 - j0 - j1) * j
        zj = s + flip * (3 - 2 * s)
        py = yy + fy * (1 - 2 * yy)
        px = xx + fx * (1 - 2 * xx)
        pid = py * 2 + px
        wait_piece(zj * NC + pid * 2 + 1 - core)
        row = pl.multiple_of(zj * group + pid * block, block)
        rows = pl.ds(row, block)
        xb = x_ref[rows, :]
        xt_ref[:, rows] = x_ref[rows, own_col].astype(jnp.float32).T.astype(jnp.bfloat16)

        def dots(c):
            bufs[c % 2][...] = lax.dot_general(
                c_ref[c * CHUNK:(c + 1) * CHUNK, :], xb, NT, preferred_element_type=jnp.float32
            )

        tops, sums = [], []

        def soft(c):
            ks = slice(c * CHUNK, (c + 1) * CHUNK)
            b = bias_ref[ks, :]
            ms, ls = [], []
            for h in range(block // 128):
                t = bufs[c % 2][:, h * 128:(h + 1) * 128] * gain - b
                m = jnp.max(t, axis=0, keepdims=True)
                e = jnp.exp2(t - m)
                ls.append(jnp.sum(e, axis=0, keepdims=True))
                ms.append(m)
                e_ref[ks, pl.ds(pl.multiple_of(row + h * 128, 128), 128)] = e.astype(jnp.bfloat16)
            m, l = jnp.concatenate(ms, axis=1), jnp.concatenate(ls, axis=1)
            mstat[pl.ds(c, 1), rows] = m
            tops.append(m)
            sums.append(l)

        dots(0)
        for c in range(n_chunk):
            if c + 1 < n_chunk:
                dots(c + 1)
            soft(c)
        top = functools.reduce(jnp.maximum, tops)
        total = sum(l * jnp.exp2(m - top) for m, l in zip(tops, sums))
        inner = pl.ds(pl.multiple_of(pid * block, block), block)
        gath[cent, zj, 0:1, inner] = top
        gath[cent, zj, 1:2, inner] = total

        for at, jj in ((4, 0), (8, 1), (12, 2), (15, 3)):
            @pl.when(n == at)
            def _(jj=jj):
                for d in range(1, NC):
                    stat_copy(jj, d).start()
        return 0

    lax.fori_loop(0, 16, step, 0)

    for d in range(1, NC):
        frm = (cent + d) % NC
        for w in range(NZ):
            pltpu.make_async_remote_copy(
                src_ref=gath.at[frm, w], dst_ref=gath.at[frm, w],
                send_sem=stat_send.at[0, 0], recv_sem=stat_recv.at[frm, w],
                device_id=sib, device_id_type=MESH,
            ).wait_recv()
    for w in range(NZ):
        cols = slice(w * group, (w + 1) * group)
        ms = [gath[q, w, 0:1, :] for q in range(NC)]
        top = functools.reduce(jnp.maximum, ms)
        total = sum(gath[q, w, 1:2, :] * jnp.exp2(ms[q] - top) for q in range(NC))
        inv = 1.0 / total
        for c in range(n_chunk):
            scale_ref[c:c + 1, cols] = jnp.exp2(mstat[c:c + 1, cols] - top) * inv

    sub = obuf.shape[2]
    n_sub = CHUNK // sub

    def out_copy(c, u):
        col = pl.multiple_of(c * CHUNK + u * sub, sub)
        return pltpu.make_async_copy(obuf.at[u], out_ref.at[:, pl.ds(col, sub)], out_sem.at[u])

    def sums_step(c, _):
        sc = scale_ref[pl.ds(c, 1), :]
        a_ref[0:own_feats, :] = (xt_ref[...].astype(jnp.float32) * sc).astype(jnp.bfloat16)
        hi = sc.astype(jnp.bfloat16).astype(jnp.float32)
        lo = sc - hi
        which = lax.broadcasted_iota(jnp.int32, (16, sc.shape[1]), 0)
        extra = jnp.where(which == 0, hi, jnp.where(which == 1, lo, 0.0))
        a_ref[own_feats:own_feats + 16, :] = extra.astype(jnp.bfloat16)
        for u in range(n_sub):
            ks = pl.ds(pl.multiple_of(c * CHUNK + u * sub, sub), sub)
            res = lax.dot_general(a_ref[...], e_ref[ks, :], NT, preferred_element_type=jnp.float32)
            counts = res[own_feats:own_feats + 1] + res[own_feats + 1:own_feats + 2]
            inv = 1.0 / (counts + PRIOR)
            own = c_ref[ks, own_col].astype(jnp.float32).T

            @pl.when(c > 0)
            def _(u=u):
                out_copy(c - 1, u).wait()

            obuf[u] = (res[:own_feats] + PRIOR * own) * inv
            out_copy(c, u).start()
        return 0

    lax.fori_loop(0, n_chunk, sums_step, 0)
    for u in range(n_sub):
        out_copy(n_chunk - 1, u).wait()
    for j in range(NZ):
        for pos in POS:
            each_route(j, pos, lambda c: c.wait_send())
        for d in range(1, NC):
            stat_copy(j, d).wait_send()


def fused_local(points, centroids):
    shard, feats = points.shape
    kc = centroids.shape[0]
    rows = shard * NZ * NC
    own = feats // NZ
    dma = pltpu.SemaphoreType.DMA
    return pl.pallas_call(
        fused,
        out_shape=jax.ShapeDtypeStruct((own, kc), jnp.float32),
        in_specs=[pl.BlockSpec(memory_space=pl.ANY)] * 2,
        out_specs=pl.BlockSpec(memory_space=pl.ANY),
        scratch_shapes=[
            pltpu.VMEM((rows, feats), jnp.bfloat16),
            pltpu.VMEM((kc, feats), jnp.bfloat16),
            pltpu.VMEM((kc, rows), jnp.bfloat16),
            pltpu.VMEM((own, rows), jnp.bfloat16),
            pltpu.VMEM((own + 16, rows), jnp.bfloat16),
            pltpu.VMEM((kc, 128), jnp.float32),
            pltpu.VMEM((CHUNK, 2 * shard), jnp.float32),
            pltpu.VMEM((CHUNK, 2 * shard), jnp.float32),
            pltpu.VMEM((2, own, CHUNK // 2), jnp.float32),
            pltpu.VMEM((kc // CHUNK, rows), jnp.float32),
            pltpu.VMEM((kc // CHUNK, rows), jnp.float32),
            pltpu.VMEM((NC, NZ, 2, NC * shard), jnp.float32),
            dma((2,)),
            dma((NZ * 4 * 5,)),
            dma((NZ * NC,)),
            dma((NZ, NC)),
            dma((NC, NZ)),
            dma((2,)),
        ],
        compiler_params=pltpu.CompilerParams(
            collective_id=0, has_side_effects=True, vmem_limit_bytes=62 * 2**20
        ),
        cost_estimate=pl.CostEstimate(
            flops=2 * rows * kc * (feats + own), bytes_accessed=2 * kc * feats + 4 * own * kc,
            transcendentals=rows * kc,
        ),
    )(points, centroids)


def solution(mesh):
    def local(points, centroids):
        small = (
            mesh.shape["dp"] == NZ and mesh.shape["cent"] == NC
            and points.shape == (128, 1024) and centroids.shape == (4096, 1024)
        )
        return fused_local(points, centroids) if small else general(points, centroids)

    return jax.shard_map(
        local,
        mesh=mesh,
        in_specs=(P(("dp", "cent"), None), P("cent", None)),
        out_specs=P("dp", "cent"),
        check_vma=False,
    )
```

```python
import functools
import math

import jax
import jax.numpy as jnp
from jax import lax
from jax.experimental import pallas as pl
from jax.experimental.pallas import tpu as pltpu
from jax.sharding import PartitionSpec as P

BETA_GAIN = 4.0
PRIOR = 0.5
MESH = pl.DeviceIdType.MESH
NT = (((1,), (1,)), ((), ()))


def general(points, centroids):
    features = points.shape[1]
    sharpness = BETA_GAIN * features ** (-0.5)
    gathered = lax.all_gather(points, "cent", axis=0, tiled=True)
    sqnorm = jnp.sum(jnp.square(centroids.astype(jnp.float32)), axis=1)
    total_rows = gathered.shape[0]
    block_rows = min(512, total_rows)
    blocks = gathered.reshape(total_rows // block_rows, block_rows, features)
    shard_cents = centroids.shape[0]

    def logits_of(xblock):
        dots = lax.dot_general(xblock, centroids, NT, preferred_element_type=jnp.float32)
        return sharpness * (dots - 0.5 * sqnorm[None, :])

    def resp_of(logits, row_top, row_total):
        return (jnp.exp(logits - row_top[:, None]) / row_total[:, None]).astype(jnp.bfloat16)

    logits = lax.map(logits_of, blocks)
    local_max = jnp.max(logits, axis=-1)
    local_sum = jnp.sum(jnp.exp(logits - local_max[..., None]), axis=-1)
    row_top = lax.pmax(local_max, "cent")
    row_total = lax.psum(local_sum * jnp.exp(local_max - row_top), "cent")
    resp = jax.vmap(resp_of)(logits, row_top, row_total)
    resp = resp.reshape(total_rows, shard_cents)
    counts = jnp.sum(resp.astype(jnp.float32), axis=0)
    dp_count = lax.axis_size("dp")
    dp_index = lax.axis_index("dp")
    column_share = features // dp_count
    numer = lax.psum_scatter(
        lax.dot_general(
            gathered, resp, (((0,), (0,)), ((), ())), preferred_element_type=jnp.float32
        ).astype(jnp.bfloat16),
        "dp",
        scatter_dimension=0,
        tiled=True,
    ).astype(jnp.float32)
    counts_all = lax.psum(counts, "dp")
    own_cols = (
        lax.dynamic_slice_in_dim(centroids, dp_index * column_share, column_share, 1)
        .astype(jnp.float32)
        .T
    )
    return (numer + PRIOR * own_cols) / (counts_all[None, :] + PRIOR)


NZ = 4
NC = 8
PIECE = 512
CHUNK = 1024


def fused(
    points_ref, cents_ref, out_ref,
    x_ref, c_ref, e_ref, xt_ref, a_ref, bias_ref, buf0, buf1, obuf, mstat, scale_ref, gath,
    load_sem, send_sem, recv_sem, stat_send, stat_recv, out_sem,
):
    shard, feats = points_ref.shape
    kc = cents_ref.shape[0]
    n_chunk = kc // CHUNK
    block = 2 * shard
    group = NC * shard
    own_feats = feats // NZ
    gain = BETA_GAIN * feats ** (-0.5) * math.log2(math.e)

    z = lax.axis_index("dp")
    cent = lax.axis_index("cent")
    core = cent % 2
    xx = (cent // 2) % 2
    yy = cent // 4
    flip = z // 2
    zz = z + flip * (3 - 2 * z)

    def z_of(j):
        s = (1 - zz) if j == 1 else (zz if j == 0 else j)
        return s + flip * (3 - 2 * s)

    def pos_of(pos):
        fx = pos in ("x", "d")
        fy = pos in ("y", "d")
        return ((1 - yy) if fy else yy) * 2 + ((1 - xx) if fx else xx)

    x_peer = (z, (yy * 2 + 1 - xx) * 2 + core)
    y_peer = (z, ((1 - yy) * 2 + xx) * 2 + core)
    sib = (z, cent + 1 - 2 * core)

    def piece(sid):
        return x_ref.at[pl.ds(pl.multiple_of(sid * shard, shard), shard)]

    def sid_of(j, pos, other=False):
        return z_of(j) * NC + pos_of(pos) * 2 + ((1 - core) if other else core)

    def copy_to(sid, dev, slot):
        return pltpu.make_async_remote_copy(
            src_ref=piece(sid), dst_ref=piece(sid), send_sem=send_sem.at[slot],
            recv_sem=recv_sem.at[sid], device_id=dev, device_id_type=MESH,
        )

    def wait_piece(sid):
        copy_to(sid, sib, 0).wait_recv()

    POS = {"c": 0, "x": 1, "y": 2, "d": 3}

    def routes(j, pos):
        base = (j * 4 + POS[pos]) * 5
        r = []
        if pos == "c":
            zj = z_of(j)
            up = (zj <= z) & (z < NZ - 1)
            down = (zj >= z) & (z > 0)
            r.append((up, (z + 1, cent), base))
            r.append((down, (z - 1, cent), base + 1))
            r.append((None, x_peer, base + 2))
            r.append((None, y_peer, base + 3))
        if pos == "x" and j % 2 == 0:
            r.append((None, y_peer, base + 3))
        if pos == "y" and j % 2 == 1:
            r.append((None, x_peer, base + 2))
        r.append((None, sib, base + 4))
        return r

    def each_route(j, pos, act):
        sid = sid_of(j, pos)
        for cond, dev, slot in routes(j, pos):
            if cond is None:
                act(copy_to(sid, dev, slot))
            else:
                @pl.when(cond)
                def _(dev=dev, slot=slot):
                    act(copy_to(sid, dev, slot))

    def pass_on(j, pos):
        if (j, pos) != (0, "c"):
            wait_piece(sid_of(j, pos))
        each_route(j, pos, lambda c: c.start())

    own_id = sid_of(0, "c")
    load_x = pltpu.make_async_copy(points_ref, piece(own_id), load_sem.at[0])
    load_c = pltpu.make_async_copy(cents_ref, c_ref, load_sem.at[1])
    load_x.start()
    load_c.start()
    barrier = pltpu.get_barrier_semaphore()
    for d in range(1, NC):
        pl.semaphore_signal(barrier, inc=1, device_id=(z, (cent + d) % NC), device_id_type=MESH)

    @pl.when(z > 0)
    def _():
        pl.semaphore_signal(barrier, inc=1, device_id=(z - 1, cent), device_id_type=MESH)

    @pl.when(z < NZ - 1)
    def _():
        pl.semaphore_signal(barrier, inc=1, device_id=(z + 1, cent), device_id_type=MESH)

    inner_z = jnp.minimum(z, 1) * jnp.minimum(NZ - 1 - z, 1)
    pl.semaphore_wait(barrier, NC + inner_z)

    load_x.wait()
    pass_on(0, "c")
    load_c.wait()

    def norm_step(r, _):
        rows = pl.ds(pl.multiple_of(r * 256, 256), 256)
        v = c_ref[rows, :].astype(jnp.float32)
        s = jnp.sum(v * v, axis=1, keepdims=True) * 0.5
        bias_ref[rows, :] = jnp.broadcast_to(s, (256, 128))
        return 0

    lax.fori_loop(0, kc // 256, norm_step, 0)

    def stat_copy(j, d):
        zj = z_of(j)
        return pltpu.make_async_remote_copy(
            src_ref=gath.at[cent, zj], dst_ref=gath.at[cent, zj],
            send_sem=stat_send.at[j, d], recv_sem=stat_recv.at[cent, zj],
            device_id=(z, (cent + d) % NC), device_id_type=MESH,
        )

    own_col = pl.ds(pl.multiple_of(z * own_feats, own_feats), own_feats)
    bufs = (buf0, buf1)
    n_piece = CHUNK // PIECE
    end = 1 - jnp.minimum(z, 1) * jnp.minimum(NZ - 1 - z, 1)

    def top8(v):
        return jnp.max(v.reshape(v.shape[0] // 8, 8, v.shape[1]), axis=0)

    def dots(c, p, xb):
        ks = slice(c * CHUNK + p * PIECE, c * CHUNK + (p + 1) * PIECE)
        v = lax.dot_general(c_ref[ks, :], xb, NT, preferred_element_type=jnp.float32)
        b = bias_ref[ks, :]
        v = v - jnp.concatenate([b] * (block // 128), axis=1)
        bufs[c % 2][p * PIECE:(p + 1) * PIECE, :] = v
        return top8(v)

    def expo(c, p, m, rows):
        v = bufs[c % 2][p * PIECE:(p + 1) * PIECE, :]
        e = jnp.exp2((v - m) * gain)
        e_ref[c * CHUNK + p * PIECE:c * CHUNK + (p + 1) * PIECE, rows] = e.astype(jnp.bfloat16)
        return jnp.sum(e.reshape(PIECE // 8, 8, block), axis=0)

    def finish(zj, pid, tops, sums):
        rows = pl.ds(pl.multiple_of(zj * group + pid * block, block), block)
        for c in range(n_chunk):
            mstat[c:c + 1, rows] = tops[c]
        top = functools.reduce(jnp.maximum, tops)
        total = sum(l * jnp.exp2((m - top) * gain) for m, l in zip(tops, sums))
        inner = pl.ds(pl.multiple_of(pid * block, block), block)
        gath[cent, zj, 0:1, inner] = top
        gath[cent, zj, 1:2, inner] = total

    def row_max(parts):
        return jnp.max(functools.reduce(jnp.maximum, parts), axis=0, keepdims=True)

    def row_sum(parts):
        return jnp.sum(sum(parts), axis=0, keepdims=True)

    def send_stats(j):
        for d in range(1, NC):
            stat_copy(j, d).start()

    def step(n, carry):
        pzj, ppid, ptops, psums = carry
        for at, items in (
            (1, ((0, "x"), (0, "y"), (1, "c"))),
            (2 + 4 * end, ((2, "c"),)),
            (4, ((0, "d"), (1, "x"), (1, "y"))),
            (5 + 5 * end, ((3, "c"),)),
            (8, ((1, "d"), (2, "x"), (2, "y"))),
            (12, ((2, "d"), (3, "x"), (3, "y"))),
            (15, ((3, "d"),)),
        ):
            @pl.when(n == at)
            def _(items=items):
                for j, pos in items:
                    pass_on(j, pos)

        g, r = n // 4, n % 4
        last = n // 15
        first = 1 - jnp.minimum(n, 1)
        r0 = 1 - jnp.minimum(r, 1)
        r3 = r // 3
        j = g - r0 + first + r3 - last
        fx = jnp.where(r == 1, 1, 0) + r0 - first + last
        fy = jnp.where(r == 2, 1, 0) + r0 - first + last
        j1 = jnp.where(j == 1, 1, 0)
        j0 = jnp.where(j == 0, 1, 0)
        s = j0 * zz + j1 * (1 - zz) + (1 - j0 - j1) * j
        zj = s + flip * (3 - 2 * s)
        py = yy + fy * (1 - 2 * yy)
        px = xx + fx * (1 - 2 * xx)
        pid = py * 2 + px
        wait_piece(zj * NC + pid * 2 + 1 - core)
        rows = pl.ds(pl.multiple_of(zj * group + pid * block, block), block)
        prows = pl.ds(pl.multiple_of(pzj * group + ppid * block, block), block)
        xb = x_ref[rows, :]

        tops, sums = [], []
        m, where = ptops[-1], prows
        for c in range(n_chunk):
            t8, s8 = [], []
            for p in range(n_piece):
                t8.append(dots(c, p, xb))
                s8.append(expo((c - 1) % n_chunk, p, m, where))
            if c == 0:
                finish(pzj, ppid, ptops, list(psums) + [row_sum(s8)])
                xt_ref[:, rows] = x_ref[rows, own_col].astype(jnp.float32).T.astype(jnp.bfloat16)
            else:
                sums.append(row_sum(s8))
            m, where = row_max(t8), rows
            tops.append(m)

        for at, jj in ((5, 0), (9, 1), (13, 2)):
            @pl.when(n == at)
            def _(jj=jj):
                send_stats(jj)
        return zj, pid, tuple(tops), tuple(sums)

    last_buf = bufs[(n_chunk - 1) % 2]
    last_buf[...] = jnp.zeros_like(last_buf)
    zero = jnp.zeros((1, block), jnp.float32)
    pzj, ppid, ptops, psums = lax.fori_loop(
        0, 16, step, (z, yy * 2 + xx, (zero,) * n_chunk, (zero,) * (n_chunk - 1))
    )
    prows = pl.ds(pl.multiple_of(pzj * group + ppid * block, block), block)
    s8 = [expo(n_chunk - 1, p, ptops[-1], prows) for p in range(n_piece)]
    finish(pzj, ppid, ptops, list(psums) + [row_sum(s8)])
    send_stats(3)

    for d in range(1, NC):
        frm = (cent + d) % NC
        for w in range(NZ):
            pltpu.make_async_remote_copy(
                src_ref=gath.at[frm, w], dst_ref=gath.at[frm, w],
                send_sem=stat_send.at[0, 0], recv_sem=stat_recv.at[frm, w],
                device_id=sib, device_id_type=MESH,
            ).wait_recv()
    for w in range(NZ):
        cols = slice(w * group, (w + 1) * group)
        ms = [gath[q, w, 0:1, :] for q in range(NC)]
        top = functools.reduce(jnp.maximum, ms)
        total = sum(gath[q, w, 1:2, :] * jnp.exp2((ms[q] - top) * gain) for q in range(NC))
        inv = 1.0 / total
        for c in range(n_chunk):
            scale_ref[c:c + 1, cols] = jnp.exp2((mstat[c:c + 1, cols] - top) * gain) * inv

    sub = obuf.shape[2]
    n_sub = CHUNK // sub

    def out_copy(c, u):
        col = pl.multiple_of(c * CHUNK + u * sub, sub)
        return pltpu.make_async_copy(obuf.at[u], out_ref.at[:, pl.ds(col, sub)], out_sem.at[u])

    def sums_step(c, _):
        sc = scale_ref[pl.ds(c, 1), :]
        a_ref[0:own_feats, :] = (xt_ref[...].astype(jnp.float32) * sc).astype(jnp.bfloat16)
        hi = sc.astype(jnp.bfloat16).astype(jnp.float32)
        lo = sc - hi
        which = lax.broadcasted_iota(jnp.int32, (16, sc.shape[1]), 0)
        extra = jnp.where(which == 0, hi, jnp.where(which == 1, lo, 0.0))
        a_ref[own_feats:own_feats + 16, :] = extra.astype(jnp.bfloat16)
        for u in range(n_sub):
            ks = pl.ds(pl.multiple_of(c * CHUNK + u * sub, sub), sub)
            res = lax.dot_general(a_ref[...], e_ref[ks, :], NT, preferred_element_type=jnp.float32)
            counts = res[own_feats:own_feats + 1] + res[own_feats + 1:own_feats + 2]
            inv = 1.0 / (counts + PRIOR)
            own = c_ref[ks, own_col].astype(jnp.float32).T

            @pl.when(c > 0)
            def _(u=u):
                out_copy(c - 1, u).wait()

            obuf[u] = (res[:own_feats] + PRIOR * own) * inv
            out_copy(c, u).start()
        return 0

    lax.fori_loop(0, n_chunk, sums_step, 0)
    for u in range(n_sub):
        out_copy(n_chunk - 1, u).wait()
    for j in range(NZ):
        for pos in POS:
            each_route(j, pos, lambda c: c.wait_send())
        for d in range(1, NC):
            stat_copy(j, d).wait_send()


def fused_local(points, centroids):
    shard, feats = points.shape
    kc = centroids.shape[0]
    rows = shard * NZ * NC
    own = feats // NZ
    dma = pltpu.SemaphoreType.DMA
    return pl.pallas_call(
        fused,
        out_shape=jax.ShapeDtypeStruct((own, kc), jnp.float32),
        in_specs=[pl.BlockSpec(memory_space=pl.ANY)] * 2,
        out_specs=pl.BlockSpec(memory_space=pl.ANY),
        scratch_shapes=[
            pltpu.VMEM((rows, feats), jnp.bfloat16),
            pltpu.VMEM((kc, feats), jnp.bfloat16),
            pltpu.VMEM((kc, rows), jnp.bfloat16),
            pltpu.VMEM((own, rows), jnp.bfloat16),
            pltpu.VMEM((own + 16, rows), jnp.bfloat16),
            pltpu.VMEM((kc, 128), jnp.float32),
            pltpu.VMEM((CHUNK, 2 * shard), jnp.float32),
            pltpu.VMEM((CHUNK, 2 * shard), jnp.float32),
            pltpu.VMEM((2, own, CHUNK // 2), jnp.float32),
            pltpu.VMEM((kc // CHUNK, rows), jnp.float32),
            pltpu.VMEM((kc // CHUNK, rows), jnp.float32),
            pltpu.VMEM((NC, NZ, 2, NC * shard), jnp.float32),
            dma((2,)),
            dma((NZ * 4 * 5,)),
            dma((NZ * NC,)),
            dma((NZ, NC)),
            dma((NC, NZ)),
            dma((2,)),
        ],
        compiler_params=pltpu.CompilerParams(
            collective_id=0, has_side_effects=True, vmem_limit_bytes=62 * 2**20
        ),
        cost_estimate=pl.CostEstimate(
            flops=2 * rows * kc * (feats + own), bytes_accessed=2 * kc * feats + 4 * own * kc,
            transcendentals=rows * kc,
        ),
    )(points, centroids)


def solution(mesh):
    def local(points, centroids):
        small = (
            mesh.shape["dp"] == NZ and mesh.shape["cent"] == NC
            and points.shape == (128, 1024) and centroids.shape == (4096, 1024)
        )
        return fused_local(points, centroids) if small else general(points, centroids)

    return jax.shard_map(
        local,
        mesh=mesh,
        in_specs=(P(("dp", "cent"), None), P("cent", None)),
        out_specs=P("dp", "cent"),
        check_vma=False,
    )
```

```python
import functools
import math

import jax
import jax.numpy as jnp
from jax import lax
from jax.experimental import pallas as pl
from jax.experimental.pallas import tpu as pltpu
from jax.sharding import PartitionSpec as P

BETA_GAIN = 4.0
PRIOR = 0.5
MESH = pl.DeviceIdType.MESH
NT = (((1,), (1,)), ((), ()))


def general(points, centroids):
    features = points.shape[1]
    sharpness = BETA_GAIN * features ** (-0.5)
    gathered = lax.all_gather(points, "cent", axis=0, tiled=True)
    sqnorm = jnp.sum(jnp.square(centroids.astype(jnp.float32)), axis=1)
    total_rows = gathered.shape[0]
    block_rows = min(512, total_rows)
    blocks = gathered.reshape(total_rows // block_rows, block_rows, features)
    shard_cents = centroids.shape[0]

    def logits_of(xblock):
        dots = lax.dot_general(xblock, centroids, NT, preferred_element_type=jnp.float32)
        return sharpness * (dots - 0.5 * sqnorm[None, :])

    def resp_of(logits, row_top, row_total):
        return (jnp.exp(logits - row_top[:, None]) / row_total[:, None]).astype(jnp.bfloat16)

    logits = lax.map(logits_of, blocks)
    local_max = jnp.max(logits, axis=-1)
    local_sum = jnp.sum(jnp.exp(logits - local_max[..., None]), axis=-1)
    row_top = lax.pmax(local_max, "cent")
    row_total = lax.psum(local_sum * jnp.exp(local_max - row_top), "cent")
    resp = jax.vmap(resp_of)(logits, row_top, row_total)
    resp = resp.reshape(total_rows, shard_cents)
    counts = jnp.sum(resp.astype(jnp.float32), axis=0)
    dp_count = lax.axis_size("dp")
    dp_index = lax.axis_index("dp")
    column_share = features // dp_count
    numer = lax.psum_scatter(
        lax.dot_general(
            gathered, resp, (((0,), (0,)), ((), ())), preferred_element_type=jnp.float32
        ).astype(jnp.bfloat16),
        "dp",
        scatter_dimension=0,
        tiled=True,
    ).astype(jnp.float32)
    counts_all = lax.psum(counts, "dp")
    own_cols = (
        lax.dynamic_slice_in_dim(centroids, dp_index * column_share, column_share, 1)
        .astype(jnp.float32)
        .T
    )
    return (numer + PRIOR * own_cols) / (counts_all[None, :] + PRIOR)


NZ = 4
NC = 8
PIECE = 512
CHUNK = 1024


def fused(
    points_ref, cents_ref, out_ref,
    x_ref, c_ref, far_ref, e_ref, xt_ref, a0_ref, a1_ref, bias_ref, buf0, buf1, buf2, obuf,
    mstat, scale_ref, gath, lone, nsend, nrecv, csend, crecv,
    load_sem, send_sem, recv_sem, stat_send, stat_recv, pair_send, pair_recv, out_sem,
):
    shard, feats = points_ref.shape
    n_chunk = cents_ref.shape[0] // CHUNK - 1
    kc = n_chunk * CHUNK
    block = 2 * shard
    group = NC * shard
    own_feats = feats // NZ
    gain = BETA_GAIN * feats ** (-0.5) * math.log2(math.e)

    z = lax.axis_index("dp")
    cent = lax.axis_index("cent")
    core = cent % 2
    xx = (cent // 2) % 2
    yy = cent // 4
    flip = z // 2
    odd = z % 2
    pz = z + 1 - 2 * odd
    lone_row = pl.multiple_of(odd * kc, CHUNK)
    far_row = pl.multiple_of((1 - odd) * kc, CHUNK)
    zz = z + flip * (3 - 2 * z)

    def z_of(j):
        s = (1 - zz) if j == 1 else (zz if j == 0 else j)
        return s + flip * (3 - 2 * s)

    def pos_of(pos):
        fx = pos in ("x", "d")
        fy = pos in ("y", "d")
        return ((1 - yy) if fy else yy) * 2 + ((1 - xx) if fx else xx)

    x_peer = (z, (yy * 2 + 1 - xx) * 2 + core)
    y_peer = (z, ((1 - yy) * 2 + xx) * 2 + core)
    sib = (z, cent + 1 - 2 * core)

    def piece(sid):
        return x_ref.at[pl.ds(pl.multiple_of(sid * shard, shard), shard)]

    def sid_of(j, pos, other=False):
        return z_of(j) * NC + pos_of(pos) * 2 + ((1 - core) if other else core)

    def copy_to(sid, dev, slot):
        return pltpu.make_async_remote_copy(
            src_ref=piece(sid), dst_ref=piece(sid), send_sem=send_sem.at[slot],
            recv_sem=recv_sem.at[sid], device_id=dev, device_id_type=MESH,
        )

    def wait_piece(sid):
        copy_to(sid, sib, 0).wait_recv()

    POS = {"c": 0, "x": 1, "y": 2, "d": 3}

    def routes(j, pos):
        base = (j * 4 + POS[pos]) * 5
        r = []
        if pos == "c":
            zj = z_of(j)
            up = (zj <= z) & (z < NZ - 1)
            down = (zj >= z) & (z > 0)
            r.append((up, (z + 1, cent), base))
            r.append((down, (z - 1, cent), base + 1))
            r.append((None, x_peer, base + 2))
            r.append((None, y_peer, base + 3))
        if pos == "x" and j % 2 == 0:
            r.append((None, y_peer, base + 3))
        if pos == "y" and j % 2 == 1:
            r.append((None, x_peer, base + 2))
        r.append((None, sib, base + 4))
        return r

    def each_route(j, pos, act):
        sid = sid_of(j, pos)
        for cond, dev, slot in routes(j, pos):
            if cond is None:
                act(copy_to(sid, dev, slot))
            else:
                @pl.when(cond)
                def _(dev=dev, slot=slot):
                    act(copy_to(sid, dev, slot))

    def pass_on(j, pos):
        if (j, pos) != (0, "c"):
            wait_piece(sid_of(j, pos))
        each_route(j, pos, lambda c: c.start())

    own_id = sid_of(0, "c")
    load_x = pltpu.make_async_copy(points_ref, piece(own_id), load_sem.at[0])
    own_col = pl.ds(pl.multiple_of(z * own_feats, own_feats), own_feats)
    pair_col = pl.ds(pl.multiple_of(pz * own_feats, own_feats), own_feats)
    loads = [
        pltpu.make_async_copy(
            cents_ref.at[pl.ds(lone_row, CHUNK)], c_ref.at[pl.ds(0, CHUNK)], load_sem.at[1]
        ),
        pltpu.make_async_copy(
            cents_ref.at[pl.ds(CHUNK, kc - CHUNK)], c_ref.at[pl.ds(CHUNK, kc - CHUNK)],
            load_sem.at[2],
        ),
        pltpu.make_async_copy(
            cents_ref.at[pl.ds(far_row, CHUNK), own_col], far_ref, load_sem.at[3]
        ),
    ]
    load_x.start()
    for c in loads:
        c.start()
    barrier = pltpu.get_barrier_semaphore()
    for d in range(1, NC):
        pl.semaphore_signal(barrier, inc=1, device_id=(z, (cent + d) % NC), device_id_type=MESH)
    for d in range(NC):
        pl.semaphore_signal(barrier, inc=1, device_id=(pz, (cent + d) % NC), device_id_type=MESH)
    inner_z = jnp.minimum(z, 1) * jnp.minimum(NZ - 1 - z, 1)

    @pl.when(inner_z == 1)
    def _():
        pl.semaphore_signal(barrier, inc=1, device_id=(3 - z, cent), device_id_type=MESH)

    pl.semaphore_wait(barrier, 2 * NC - 1 + inner_z)

    load_x.wait()
    pass_on(0, "c")
    for c in loads:
        c.wait()

    def norm_step(r, _):
        rows = pl.ds(pl.multiple_of(r * 256, 256), 256)
        v = c_ref[rows, :].astype(jnp.float32)
        s = jnp.sum(v * v, axis=1, keepdims=True) * 0.5
        bias_ref[rows, :] = jnp.broadcast_to(s, (256, 128))
        return 0

    lax.fori_loop(0, kc // 256, norm_step, 0)

    def stat_copy(j, d):
        zj = z_of(j)
        if d < NC:
            src, slot, dev = gath.at[cent, zj], cent, (z, (cent + d) % NC)
        else:
            src, slot, dev = lone.at[zj], cent + NC, (pz, (cent + d) % NC)
        return pltpu.make_async_remote_copy(
            src_ref=src, dst_ref=gath.at[slot, zj],
            send_sem=stat_send.at[j, d], recv_sem=stat_recv.at[slot, zj],
            device_id=dev, device_id_type=MESH,
        )

    bufs = (buf0, buf1, buf2)
    n_piece = CHUNK // PIECE
    end = 1 - inner_z

    def top8(v):
        return jnp.max(v.reshape(v.shape[0] // 8, 8, v.shape[1]), axis=0)

    def dots(c, p, xb):
        ks = slice(c * CHUNK + p * PIECE, c * CHUNK + (p + 1) * PIECE)
        v = lax.dot_general(c_ref[ks, :], xb, NT, preferred_element_type=jnp.float32)
        b = bias_ref[ks, :]
        v = v - jnp.concatenate([b] * (block // 128), axis=1)
        bufs[c][p * PIECE:(p + 1) * PIECE, :] = v
        return top8(v)

    def expo(c, p, m, rows):
        v = bufs[c][p * PIECE:(p + 1) * PIECE, :]
        e = jnp.exp2((v - m) * gain)
        e_ref[c * CHUNK + p * PIECE:c * CHUNK + (p + 1) * PIECE, rows] = e.astype(jnp.bfloat16)
        return jnp.sum(e.reshape(PIECE // 8, 8, block), axis=0)

    def finish(zj, pid, tops, sums):
        rows = pl.ds(pl.multiple_of(zj * group + pid * block, block), block)
        for c in range(n_chunk):
            mstat[c:c + 1, rows] = tops[c]
        top = functools.reduce(jnp.maximum, tops)
        total = sum(l * jnp.exp2((m - top) * gain) for m, l in zip(tops, sums))
        inner = pl.ds(pl.multiple_of(pid * block, block), block)
        gath[cent, zj, 0:1, inner] = top
        gath[cent, zj, 1:2, inner] = total
        lone[zj, 0:1, inner] = tops[0]
        lone[zj, 1:2, inner] = sums[0]

    def row_max(parts):
        return jnp.max(functools.reduce(jnp.maximum, parts), axis=0, keepdims=True)

    def row_sum(parts):
        return jnp.sum(sum(parts), axis=0, keepdims=True)

    def send_stats(j):
        for d in range(1, 2 * NC):
            stat_copy(j, d).start()

    def step(n, carry):
        pzj, ppid, ptops, psums = carry
        for at, items in (
            (1, ((0, "x"), (0, "y"), (1, "c"))),
            (2 + 4 * end, ((2, "c"),)),
            (4, ((0, "d"), (1, "x"), (1, "y"))),
            (5 + 5 * end, ((3, "c"),)),
            (8, ((1, "d"), (2, "x"), (2, "y"))),
            (12, ((2, "d"), (3, "x"), (3, "y"))),
            (15, ((3, "d"),)),
        ):
            @pl.when(n == at)
            def _(items=items):
                for j, pos in items:
                    pass_on(j, pos)

        g, r = n // 4, n % 4
        last = n // 15
        first = 1 - jnp.minimum(n, 1)
        r0 = 1 - jnp.minimum(r, 1)
        r3 = r // 3
        j = g - r0 + first + r3 - last
        fx = jnp.where(r == 1, 1, 0) + r0 - first + last
        fy = jnp.where(r == 2, 1, 0) + r0 - first + last
        j1 = jnp.where(j == 1, 1, 0)
        j0 = jnp.where(j == 0, 1, 0)
        s = j0 * zz + j1 * (1 - zz) + (1 - j0 - j1) * j
        zj = s + flip * (3 - 2 * s)
        py = yy + fy * (1 - 2 * yy)
        px = xx + fx * (1 - 2 * xx)
        pid = py * 2 + px
        wait_piece(zj * NC + pid * 2 + 1 - core)
        rows = pl.ds(pl.multiple_of(zj * group + pid * block, block), block)
        prows = pl.ds(pl.multiple_of(pzj * group + ppid * block, block), block)
        xb = x_ref[rows, :]

        tops, sums = [], []
        m, where = ptops[-1], prows
        for c in range(n_chunk):
            t8, s8 = [], []
            for p in range(n_piece):
                t8.append(dots(c, p, xb))
                s8.append(expo((c - 1) % n_chunk, p, m, where))
            if c == 0:
                finish(pzj, ppid, ptops, list(psums) + [row_sum(s8)])
                for half, cols in enumerate((own_col, pair_col)):
                    xt = x_ref[rows, cols].astype(jnp.float32).T.astype(jnp.bfloat16)
                    xt_ref[half * own_feats:(half + 1) * own_feats, rows] = xt
            else:
                sums.append(row_sum(s8))
            m, where = row_max(t8), rows
            tops.append(m)

        for at, jj in ((5, 0), (9, 1), (13, 2)):
            @pl.when(n == at)
            def _(jj=jj):
                send_stats(jj)
        return zj, pid, tuple(tops), tuple(sums)

    last_buf = bufs[n_chunk - 1]
    last_buf[...] = jnp.zeros_like(last_buf)
    zero = jnp.zeros((1, block), jnp.float32)
    pzj, ppid, ptops, psums = lax.fori_loop(
        0, 16, step, (z, yy * 2 + xx, (zero,) * n_chunk, (zero,) * (n_chunk - 1))
    )
    prows = pl.ds(pl.multiple_of(pzj * group + ppid * block, block), block)
    s8 = [expo(n_chunk - 1, p, ptops[-1], prows) for p in range(n_piece)]
    finish(pzj, ppid, ptops, list(psums) + [row_sum(s8)])
    send_stats(3)

    for d in range(1, 2 * NC):
        frm = (cent + d) % NC + (NC if d >= NC else 0)
        for w in range(NZ):
            pltpu.make_async_remote_copy(
                src_ref=gath.at[frm, w], dst_ref=gath.at[frm, w],
                send_sem=stat_send.at[0, 0], recv_sem=stat_recv.at[frm, w],
                device_id=sib, device_id_type=MESH,
            ).wait_recv()
    for w in range(NZ):
        cols = slice(w * group, (w + 1) * group)
        ms = [gath[q, w, 0:1, :] for q in range(2 * NC)]
        top = functools.reduce(jnp.maximum, ms)
        total = sum(
            gath[q, w, 1:2, :] * jnp.exp2((ms[q] - top) * gain) for q in range(2 * NC)
        )
        inv = 1.0 / total
        for c in range(n_chunk):
            scale_ref[c:c + 1, cols] = jnp.exp2((mstat[c:c + 1, cols] - top) * gain) * inv

    sub = obuf.shape[2]
    n_sub = CHUNK // sub
    slots = obuf.shape[0]
    a_refs = (a0_ref, a1_ref)
    writes = []

    def write(value, row):
        t = len(writes)
        if t >= slots:
            writes[t - slots].wait()
        obuf[t % slots] = value
        copy = pltpu.make_async_copy(
            obuf.at[t % slots], out_ref.at[:, pl.ds(row, sub)], out_sem.at[t % slots]
        )
        copy.start()
        writes.append(copy)

    def pair_copies(u):
        return [
            pltpu.make_async_remote_copy(
                src_ref=src.at[u], dst_ref=dst.at[u], send_sem=pair_send.at[i, u],
                recv_sem=pair_recv.at[i, u], device_id=(pz, cent), device_id_type=MESH,
            )
            for i, (src, dst) in enumerate(((nsend, nrecv), (csend, crecv)))
        ]

    def prepare(c):
        feats_here = own_feats * (2 if c == 0 else 1)
        a = a_refs[c % 2]
        sc = scale_ref[c:c + 1, :]
        a[0:feats_here, :] = (xt_ref[0:feats_here, :].astype(jnp.float32) * sc).astype(jnp.bfloat16)
        hi = sc.astype(jnp.bfloat16).astype(jnp.float32)
        which = lax.broadcasted_iota(jnp.int32, (16, sc.shape[1]), 0)
        extra = jnp.where(which == 0, hi, jnp.where(which == 1, sc - hi, 0.0))
        a[feats_here:feats_here + 16, :] = extra.astype(jnp.bfloat16)

    def multiply(c, u):
        height = own_feats * (2 if c == 0 else 1)
        ks = slice(c * CHUNK + u * sub, c * CHUNK + (u + 1) * sub)
        res = lax.dot_general(
            a_refs[c % 2][0:height + 16, :], e_ref[ks, :], NT, preferred_element_type=jnp.float32
        )
        counts = res[height:height + 1] + res[height + 1:height + 2]
        if c == 0:
            nsend[u] = res[own_feats:height].astype(jnp.bfloat16)
            csend[u] = jnp.broadcast_to(counts, csend.shape[1:])
            for copy in pair_copies(u):
                copy.start()
        return res[:own_feats], counts

    def conclude(c, u, numer, counts):
        ks = slice(c * CHUNK + u * sub, c * CHUNK + (u + 1) * sub)
        own = c_ref[ks, own_col].astype(jnp.float32).T
        base = lone_row if c == 0 else c * CHUNK
        write((numer + PRIOR * own) * (1.0 / (counts + PRIOR)), base + u * sub)

    prepare(0)
    pending = None
    for c in range(n_chunk):
        for u in range(n_sub):
            done = multiply(c, u)
            if u == 0 and c + 1 < n_chunk:
                prepare(c + 1)
            if pending is not None:
                conclude(*pending)
            pending = (c, u, *done)
    conclude(*pending)
    for u in range(n_sub):
        for copy in pair_copies(u):
            copy.wait_recv()
        own = far_ref[u * sub:(u + 1) * sub, :].astype(jnp.float32).T
        counts = crecv[u][0:1]
        write(
            (nrecv[u].astype(jnp.float32) + PRIOR * own) * (1.0 / (counts + PRIOR)),
            pl.multiple_of(far_row + u * sub, sub),
        )
    for copy in writes[-slots:]:
        copy.wait()
    for u in range(n_sub):
        for copy in pair_copies(u):
            copy.wait_send()
    for j in range(NZ):
        for pos in POS:
            each_route(j, pos, lambda c: c.wait_send())
        for d in range(1, 2 * NC):
            stat_copy(j, d).wait_send()


def fused_local(points, centroids):
    shard, feats = points.shape
    all_kc = centroids.shape[0]
    kc = all_kc - CHUNK
    half = CHUNK // 2
    rows = shard * NZ * NC
    own = feats // NZ
    dma = pltpu.SemaphoreType.DMA
    return pl.pallas_call(
        fused,
        out_shape=jax.ShapeDtypeStruct((own, all_kc), jnp.float32),
        in_specs=[pl.BlockSpec(memory_space=pl.ANY)] * 2,
        out_specs=pl.BlockSpec(memory_space=pl.ANY),
        scratch_shapes=[
            pltpu.VMEM((rows, feats), jnp.bfloat16),
            pltpu.VMEM((kc, feats), jnp.bfloat16),
            pltpu.VMEM((CHUNK, own), jnp.bfloat16),
            pltpu.VMEM((kc, rows), jnp.bfloat16),
            pltpu.VMEM((2 * own, rows), jnp.bfloat16),
            pltpu.VMEM((2 * own + 16, rows), jnp.bfloat16),
            pltpu.VMEM((own + 16, rows), jnp.bfloat16),
            pltpu.VMEM((kc, 128), jnp.float32),
            pltpu.VMEM((CHUNK, 2 * shard), jnp.float32),
            pltpu.VMEM((CHUNK, 2 * shard), jnp.float32),
            pltpu.VMEM((CHUNK, 2 * shard), jnp.float32),
            pltpu.VMEM((4, own, half), jnp.float32),
            pltpu.VMEM((kc // CHUNK, rows), jnp.float32),
            pltpu.VMEM((kc // CHUNK, rows), jnp.float32),
            pltpu.VMEM((2 * NC, NZ, 2, NC * shard), jnp.float32),
            pltpu.VMEM((NZ, 2, NC * shard), jnp.float32),
            pltpu.VMEM((2, own, half), jnp.bfloat16),
            pltpu.VMEM((2, own, half), jnp.bfloat16),
            pltpu.VMEM((2, 8, half), jnp.float32),
            pltpu.VMEM((2, 8, half), jnp.float32),
            dma((4,)),
            dma((NZ * 4 * 5,)),
            dma((NZ * NC,)),
            dma((NZ, 2 * NC)),
            dma((2 * NC, NZ)),
            dma((2, 2)),
            dma((2, 2)),
            dma((4,)),
        ],
        compiler_params=pltpu.CompilerParams(
            collective_id=0, has_side_effects=True, vmem_limit_bytes=62 * 2**20
        ),
        cost_estimate=pl.CostEstimate(
            flops=2 * rows * kc * (feats + own), bytes_accessed=2 * kc * feats + 4 * own * kc,
            transcendentals=rows * kc,
        ),
    )(points, centroids)


def solution(mesh):
    def local(points, centroids):
        small = (
            mesh.shape["dp"] == NZ and mesh.shape["cent"] == NC
            and points.shape == (128, 1024) and centroids.shape == (4096, 1024)
        )
        return fused_local(points, centroids) if small else general(points, centroids)

    return jax.shard_map(
        local,
        mesh=mesh,
        in_specs=(P(("dp", "cent"), None), P("cent", None)),
        out_specs=P("dp", "cent"),
        check_vma=False,
    )
```

```python
import functools
import math

import jax
import jax.numpy as jnp
from jax import lax
from jax.experimental import pallas as pl
from jax.experimental.pallas import tpu as pltpu
from jax.sharding import PartitionSpec as P

BETA_GAIN = 4.0
PRIOR = 0.5
MESH = pl.DeviceIdType.MESH
NT = (((1,), (1,)), ((), ()))


def general(points, centroids):
    features = points.shape[1]
    sharpness = BETA_GAIN * features ** (-0.5)
    gathered = lax.all_gather(points, "cent", axis=0, tiled=True)
    sqnorm = jnp.sum(jnp.square(centroids.astype(jnp.float32)), axis=1)
    total_rows = gathered.shape[0]
    block_rows = min(512, total_rows)
    blocks = gathered.reshape(total_rows // block_rows, block_rows, features)
    shard_cents = centroids.shape[0]

    def logits_of(xblock):
        dots = lax.dot_general(xblock, centroids, NT, preferred_element_type=jnp.float32)
        return sharpness * (dots - 0.5 * sqnorm[None, :])

    def resp_of(logits, row_top, row_total):
        return (jnp.exp(logits - row_top[:, None]) / row_total[:, None]).astype(jnp.bfloat16)

    logits = lax.map(logits_of, blocks)
    local_max = jnp.max(logits, axis=-1)
    local_sum = jnp.sum(jnp.exp(logits - local_max[..., None]), axis=-1)
    row_top = lax.pmax(local_max, "cent")
    row_total = lax.psum(local_sum * jnp.exp(local_max - row_top), "cent")
    resp = jax.vmap(resp_of)(logits, row_top, row_total)
    resp = resp.reshape(total_rows, shard_cents)
    counts = jnp.sum(resp.astype(jnp.float32), axis=0)
    dp_count = lax.axis_size("dp")
    dp_index = lax.axis_index("dp")
    column_share = features // dp_count
    numer = lax.psum_scatter(
        lax.dot_general(
            gathered, resp, (((0,), (0,)), ((), ())), preferred_element_type=jnp.float32
        ).astype(jnp.bfloat16),
        "dp",
        scatter_dimension=0,
        tiled=True,
    ).astype(jnp.float32)
    counts_all = lax.psum(counts, "dp")
    own_cols = (
        lax.dynamic_slice_in_dim(centroids, dp_index * column_share, column_share, 1)
        .astype(jnp.float32)
        .T
    )
    return (numer + PRIOR * own_cols) / (counts_all[None, :] + PRIOR)


NZ = 4
NC = 8
PIECE = 512
CHUNK = 1024


ORDER = (
    "c0", "x0", "y0", "c1", "x1", "c2", "y1", "d0",
    "x2", "c3", "y2", "x3", "d1", "y3", "d2", "d3",
)
DIGITS = tuple(
    tuple(
        sum(f(b) << (2 * i) for i, b in enumerate(ORDER[h:h + 8])) for h in (0, 8)
    )
    for f in (lambda b: int(b[1]), lambda b: int(b[0] in "xd"), lambda b: int(b[0] in "yd"))
)


def order_digit(k, n):
    return (jnp.where(n < 8, DIGITS[k][0], DIGITS[k][1]) >> (2 * (n % 8))) % 4


def fused(
    points_ref, cents_ref, out_ref,
    x_ref, c_ref, far_ref, e_ref, xt_ref, a0_ref, a1_ref, bias_ref, buf0, buf1, buf2, obuf,
    mstat, scale_ref, gath, lone, nsend, nrecv, csend, crecv,
    load_sem, send_sem, recv_sem, stat_send, stat_recv, pair_send, pair_recv, out_sem,
):
    shard, feats = points_ref.shape
    n_chunk = cents_ref.shape[0] // CHUNK - 1
    kc = n_chunk * CHUNK
    block = 2 * shard
    group = NC * shard
    own_feats = feats // NZ
    gain = BETA_GAIN * feats ** (-0.5) * math.log2(math.e)

    z = lax.axis_index("dp")
    cent = lax.axis_index("cent")
    core = cent % 2
    xx = (cent // 2) % 2
    yy = cent // 4
    flip = z // 2
    odd = z % 2
    pz = z + 1 - 2 * odd
    lone_row = pl.multiple_of(odd * kc, CHUNK)
    far_row = pl.multiple_of((1 - odd) * kc, CHUNK)
    zz = z + flip * (3 - 2 * z)

    def z_of(j):
        s = (1 - zz) if j == 1 else (zz if j == 0 else j)
        return s + flip * (3 - 2 * s)

    def pos_of(pos):
        fx = pos in ("x", "d")
        fy = pos in ("y", "d")
        return ((1 - yy) if fy else yy) * 2 + ((1 - xx) if fx else xx)

    x_peer = (z, (yy * 2 + 1 - xx) * 2 + core)
    y_peer = (z, ((1 - yy) * 2 + xx) * 2 + core)
    sib = (z, cent + 1 - 2 * core)

    def piece(sid):
        return x_ref.at[pl.ds(pl.multiple_of(sid * shard, shard), shard)]

    def sid_of(j, pos, other=False):
        return z_of(j) * NC + pos_of(pos) * 2 + ((1 - core) if other else core)

    def copy_to(sid, dev, slot):
        return pltpu.make_async_remote_copy(
            src_ref=piece(sid), dst_ref=piece(sid), send_sem=send_sem.at[slot],
            recv_sem=recv_sem.at[sid], device_id=dev, device_id_type=MESH,
        )

    def wait_piece(sid):
        copy_to(sid, sib, 0).wait_recv()

    POS = {"c": 0, "x": 1, "y": 2, "d": 3}

    def routes(j, pos):
        base = (j * 4 + POS[pos]) * 5
        r = []
        if pos == "c":
            zj = z_of(j)
            up = (zj <= z) & (z < NZ - 1)
            down = (zj >= z) & (z > 0)
            r.append((up, (z + 1, cent), base))
            r.append((down, (z - 1, cent), base + 1))
            r.append((None, x_peer, base + 2))
            r.append((None, y_peer, base + 3))
        if pos == "x" and j % 2 == 0:
            r.append((None, y_peer, base + 3))
        if pos == "y" and j % 2 == 1:
            r.append((None, x_peer, base + 2))
        r.append((None, sib, base + 4))
        return r

    def each_route(j, pos, act):
        sid = sid_of(j, pos)
        for cond, dev, slot in routes(j, pos):
            if cond is None:
                act(copy_to(sid, dev, slot))
            else:
                @pl.when(cond)
                def _(dev=dev, slot=slot):
                    act(copy_to(sid, dev, slot))

    def pass_on(j, pos):
        if (j, pos) != (0, "c"):
            wait_piece(sid_of(j, pos))
        each_route(j, pos, lambda c: c.start())

    own_id = sid_of(0, "c")
    load_x = pltpu.make_async_copy(points_ref, piece(own_id), load_sem.at[0])
    own_col = pl.ds(pl.multiple_of(z * own_feats, own_feats), own_feats)
    pair_col = pl.ds(pl.multiple_of(pz * own_feats, own_feats), own_feats)
    loads = [
        pltpu.make_async_copy(
            cents_ref.at[pl.ds(lone_row, CHUNK)], c_ref.at[pl.ds(0, CHUNK)], load_sem.at[1]
        ),
        pltpu.make_async_copy(
            cents_ref.at[pl.ds(CHUNK, kc - CHUNK)], c_ref.at[pl.ds(CHUNK, kc - CHUNK)],
            load_sem.at[2],
        ),
        pltpu.make_async_copy(
            cents_ref.at[pl.ds(far_row, CHUNK), own_col], far_ref, load_sem.at[3]
        ),
    ]
    load_x.start()
    for c in loads:
        c.start()
    barrier = pltpu.get_barrier_semaphore()
    for d in range(1, NC):
        pl.semaphore_signal(barrier, inc=1, device_id=(z, (cent + d) % NC), device_id_type=MESH)
    for d in range(NC):
        pl.semaphore_signal(barrier, inc=1, device_id=(pz, (cent + d) % NC), device_id_type=MESH)
    inner_z = jnp.minimum(z, 1) * jnp.minimum(NZ - 1 - z, 1)

    @pl.when(inner_z == 1)
    def _():
        pl.semaphore_signal(barrier, inc=1, device_id=(3 - z, cent), device_id_type=MESH)

    pl.semaphore_wait(barrier, 2 * NC - 1 + inner_z)

    load_x.wait()
    pass_on(0, "c")
    for c in loads:
        c.wait()

    def norm_step(r, _):
        rows = pl.ds(pl.multiple_of(r * 256, 256), 256)
        v = c_ref[rows, :].astype(jnp.float32)
        s = jnp.sum(v * v, axis=1, keepdims=True) * 0.5
        bias_ref[rows, :] = jnp.broadcast_to(s, (256, 128))
        return 0

    lax.fori_loop(0, kc // 256, norm_step, 0)

    def stat_copy(j, d):
        zj = z_of(j)
        if d < NC:
            src, slot, dev = gath.at[cent, zj], cent, (z, (cent + d) % NC)
        else:
            src, slot, dev = lone.at[zj], cent + NC, (pz, (cent + d) % NC)
        return pltpu.make_async_remote_copy(
            src_ref=src, dst_ref=gath.at[slot, zj],
            send_sem=stat_send.at[j, d], recv_sem=stat_recv.at[slot, zj],
            device_id=dev, device_id_type=MESH,
        )

    bufs = (buf0, buf1, buf2)
    n_piece = CHUNK // PIECE
    end = 1 - inner_z

    def top8(v):
        return jnp.max(v.reshape(v.shape[0] // 8, 8, v.shape[1]), axis=0)

    def dots(c, p, xb):
        ks = slice(c * CHUNK + p * PIECE, c * CHUNK + (p + 1) * PIECE)
        v = lax.dot_general(c_ref[ks, :], xb, NT, preferred_element_type=jnp.float32)
        b = bias_ref[ks, :]
        v = v - jnp.concatenate([b] * (block // 128), axis=1)
        bufs[c][p * PIECE:(p + 1) * PIECE, :] = v
        return top8(v)

    def expo(c, p, m, rows):
        v = bufs[c][p * PIECE:(p + 1) * PIECE, :]
        e = jnp.exp2((v - m) * gain)
        e_ref[c * CHUNK + p * PIECE:c * CHUNK + (p + 1) * PIECE, rows] = e.astype(jnp.bfloat16)
        return jnp.sum(e.reshape(PIECE // 8, 8, block), axis=0)

    def finish(zj, pid, tops, sums):
        rows = pl.ds(pl.multiple_of(zj * group + pid * block, block), block)
        for c in range(n_chunk):
            mstat[c:c + 1, rows] = tops[c]
        top = functools.reduce(jnp.maximum, tops)
        total = sum(l * jnp.exp2((m - top) * gain) for m, l in zip(tops, sums))
        inner = pl.ds(pl.multiple_of(pid * block, block), block)
        gath[cent, zj, 0:1, inner] = top
        gath[cent, zj, 1:2, inner] = total
        lone[zj, 0:1, inner] = tops[0]
        lone[zj, 1:2, inner] = sums[0]

    def row_max(parts):
        return jnp.max(functools.reduce(jnp.maximum, parts), axis=0, keepdims=True)

    def row_sum(parts):
        return jnp.sum(sum(parts), axis=0, keepdims=True)

    def send_stats(j):
        for d in range(1, 2 * NC):
            stat_copy(j, d).start()

    def step(n, carry):
        pzj, ppid, ptops, psums = carry
        for at, items in (
            (1, ((0, "x"), (0, "y"), (1, "c"))),
            (1 + 2 * end, ((2, "c"),)),
            (3, ((1, "x"),)),
            (3 + 2 * end, ((3, "c"),)),
            (5, ((1, "y"), (0, "d"), (2, "x"))),
            (7, ((2, "y"),)),
            (9, ((3, "x"), (1, "d"))),
            (11, ((3, "y"), (2, "d"))),
            (14, ((3, "d"),)),
        ):
            @pl.when(n == at)
            def _(items=items):
                for j, pos in items:
                    pass_on(j, pos)

        j, fx, fy = (order_digit(k, n) for k in range(3))
        j1 = jnp.where(j == 1, 1, 0)
        j0 = jnp.where(j == 0, 1, 0)
        s = j0 * zz + j1 * (1 - zz) + (1 - j0 - j1) * j
        zj = s + flip * (3 - 2 * s)
        py = yy + fy * (1 - 2 * yy)
        px = xx + fx * (1 - 2 * xx)
        pid = py * 2 + px
        wait_piece(zj * NC + pid * 2 + 1 - core)
        rows = pl.ds(pl.multiple_of(zj * group + pid * block, block), block)
        prows = pl.ds(pl.multiple_of(pzj * group + ppid * block, block), block)
        xb = x_ref[rows, :]

        tops, sums = [], []
        m, where = ptops[-1], prows
        for c in range(n_chunk):
            t8, s8 = [], []
            for p in range(n_piece):
                t8.append(dots(c, p, xb))
                s8.append(expo((c - 1) % n_chunk, p, m, where))
            if c == 0:
                finish(pzj, ppid, ptops, list(psums) + [row_sum(s8)])
                for half, cols in enumerate((own_col, pair_col)):
                    xt = x_ref[rows, cols].astype(jnp.float32).T.astype(jnp.bfloat16)
                    xt_ref[half * own_feats:(half + 1) * own_feats, rows] = xt
            else:
                sums.append(row_sum(s8))
            m, where = row_max(t8), rows
            tops.append(m)

        for at, jj in ((8, 0), (13, 1), (15, 2)):
            @pl.when(n == at)
            def _(jj=jj):
                send_stats(jj)
        return zj, pid, tuple(tops), tuple(sums)

    last_buf = bufs[n_chunk - 1]
    last_buf[...] = jnp.zeros_like(last_buf)
    zero = jnp.zeros((1, block), jnp.float32)
    pzj, ppid, ptops, psums = lax.fori_loop(
        0, 16, step, (z, yy * 2 + xx, (zero,) * n_chunk, (zero,) * (n_chunk - 1))
    )
    prows = pl.ds(pl.multiple_of(pzj * group + ppid * block, block), block)
    s8 = [expo(n_chunk - 1, p, ptops[-1], prows) for p in range(n_piece)]
    finish(pzj, ppid, ptops, list(psums) + [row_sum(s8)])
    send_stats(3)

    for d in range(1, 2 * NC):
        frm = (cent + d) % NC + (NC if d >= NC else 0)
        for w in range(NZ):
            pltpu.make_async_remote_copy(
                src_ref=gath.at[frm, w], dst_ref=gath.at[frm, w],
                send_sem=stat_send.at[0, 0], recv_sem=stat_recv.at[frm, w],
                device_id=sib, device_id_type=MESH,
            ).wait_recv()
    for w in range(NZ):
        cols = slice(w * group, (w + 1) * group)
        ms = [gath[q, w, 0:1, :] for q in range(2 * NC)]
        top = functools.reduce(jnp.maximum, ms)
        total = sum(
            gath[q, w, 1:2, :] * jnp.exp2((ms[q] - top) * gain) for q in range(2 * NC)
        )
        inv = 1.0 / total
        for c in range(n_chunk):
            scale_ref[c:c + 1, cols] = jnp.exp2((mstat[c:c + 1, cols] - top) * gain) * inv

    sub = obuf.shape[2]
    n_sub = CHUNK // sub
    slots = obuf.shape[0]
    a_refs = (a0_ref, a1_ref)
    writes = []

    def write(value, row):
        t = len(writes)
        if t >= slots:
            writes[t - slots].wait()
        obuf[t % slots] = value
        copy = pltpu.make_async_copy(
            obuf.at[t % slots], out_ref.at[:, pl.ds(row, sub)], out_sem.at[t % slots]
        )
        copy.start()
        writes.append(copy)

    def pair_copies(u):
        return [
            pltpu.make_async_remote_copy(
                src_ref=src.at[u], dst_ref=dst.at[u], send_sem=pair_send.at[i, u],
                recv_sem=pair_recv.at[i, u], device_id=(pz, cent), device_id_type=MESH,
            )
            for i, (src, dst) in enumerate(((nsend, nrecv), (csend, crecv)))
        ]

    def prepare(c):
        feats_here = own_feats * (2 if c == 0 else 1)
        a = a_refs[c % 2]
        sc = scale_ref[c:c + 1, :]
        a[0:feats_here, :] = (xt_ref[0:feats_here, :].astype(jnp.float32) * sc).astype(jnp.bfloat16)
        hi = sc.astype(jnp.bfloat16).astype(jnp.float32)
        which = lax.broadcasted_iota(jnp.int32, (16, sc.shape[1]), 0)
        extra = jnp.where(which == 0, hi, jnp.where(which == 1, sc - hi, 0.0))
        a[feats_here:feats_here + 16, :] = extra.astype(jnp.bfloat16)

    def multiply(c, u):
        height = own_feats * (2 if c == 0 else 1)
        ks = slice(c * CHUNK + u * sub, c * CHUNK + (u + 1) * sub)
        res = lax.dot_general(
            a_refs[c % 2][0:height + 16, :], e_ref[ks, :], NT, preferred_element_type=jnp.float32
        )
        counts = res[height:height + 1] + res[height + 1:height + 2]
        if c == 0:
            nsend[u] = res[own_feats:height].astype(jnp.bfloat16)
            csend[u] = jnp.broadcast_to(counts, csend.shape[1:])
            for copy in pair_copies(u):
                copy.start()
        return res[:own_feats], counts

    def conclude(c, u, numer, counts):
        ks = slice(c * CHUNK + u * sub, c * CHUNK + (u + 1) * sub)
        own = c_ref[ks, own_col].astype(jnp.float32).T
        base = lone_row if c == 0 else c * CHUNK
        write((numer + PRIOR * own) * (1.0 / (counts + PRIOR)), base + u * sub)

    prepare(0)
    pending = None
    for c in range(n_chunk):
        for u in range(n_sub):
            done = multiply(c, u)
            if u == 0 and c + 1 < n_chunk:
                prepare(c + 1)
            if pending is not None:
                conclude(*pending)
            pending = (c, u, *done)
    conclude(*pending)
    for u in range(n_sub):
        for copy in pair_copies(u):
            copy.wait_recv()
        own = far_ref[u * sub:(u + 1) * sub, :].astype(jnp.float32).T
        counts = crecv[u][0:1]
        write(
            (nrecv[u].astype(jnp.float32) + PRIOR * own) * (1.0 / (counts + PRIOR)),
            pl.multiple_of(far_row + u * sub, sub),
        )
    for copy in writes[-slots:]:
        copy.wait()
    for u in range(n_sub):
        for copy in pair_copies(u):
            copy.wait_send()
    for j in range(NZ):
        for pos in POS:
            each_route(j, pos, lambda c: c.wait_send())
        for d in range(1, 2 * NC):
            stat_copy(j, d).wait_send()


def fused_local(points, centroids):
    shard, feats = points.shape
    all_kc = centroids.shape[0]
    kc = all_kc - CHUNK
    half = CHUNK // 2
    rows = shard * NZ * NC
    own = feats // NZ
    dma = pltpu.SemaphoreType.DMA
    return pl.pallas_call(
        fused,
        out_shape=jax.ShapeDtypeStruct((own, all_kc), jnp.float32),
        in_specs=[pl.BlockSpec(memory_space=pl.ANY)] * 2,
        out_specs=pl.BlockSpec(memory_space=pl.ANY),
        scratch_shapes=[
            pltpu.VMEM((rows, feats), jnp.bfloat16),
            pltpu.VMEM((kc, feats), jnp.bfloat16),
            pltpu.VMEM((CHUNK, own), jnp.bfloat16),
            pltpu.VMEM((kc, rows), jnp.bfloat16),
            pltpu.VMEM((2 * own, rows), jnp.bfloat16),
            pltpu.VMEM((2 * own + 16, rows), jnp.bfloat16),
            pltpu.VMEM((own + 16, rows), jnp.bfloat16),
            pltpu.VMEM((kc, 128), jnp.float32),
            pltpu.VMEM((CHUNK, 2 * shard), jnp.float32),
            pltpu.VMEM((CHUNK, 2 * shard), jnp.float32),
            pltpu.VMEM((CHUNK, 2 * shard), jnp.float32),
            pltpu.VMEM((4, own, half), jnp.float32),
            pltpu.VMEM((kc // CHUNK, rows), jnp.float32),
            pltpu.VMEM((kc // CHUNK, rows), jnp.float32),
            pltpu.VMEM((2 * NC, NZ, 2, NC * shard), jnp.float32),
            pltpu.VMEM((NZ, 2, NC * shard), jnp.float32),
            pltpu.VMEM((2, own, half), jnp.bfloat16),
            pltpu.VMEM((2, own, half), jnp.bfloat16),
            pltpu.VMEM((2, 8, half), jnp.float32),
            pltpu.VMEM((2, 8, half), jnp.float32),
            dma((4,)),
            dma((NZ * 4 * 5,)),
            dma((NZ * NC,)),
            dma((NZ, 2 * NC)),
            dma((2 * NC, NZ)),
            dma((2, 2)),
            dma((2, 2)),
            dma((4,)),
        ],
        compiler_params=pltpu.CompilerParams(
            collective_id=0, has_side_effects=True, vmem_limit_bytes=62 * 2**20
        ),
        cost_estimate=pl.CostEstimate(
            flops=2 * rows * kc * (feats + own), bytes_accessed=2 * kc * feats + 4 * own * kc,
            transcendentals=rows * kc,
        ),
    )(points, centroids)


def solution(mesh):
    def local(points, centroids):
        small = (
            mesh.shape["dp"] == NZ and mesh.shape["cent"] == NC
            and points.shape == (128, 1024) and centroids.shape == (4096, 1024)
        )
        return fused_local(points, centroids) if small else general(points, centroids)

    return jax.shard_map(
        local,
        mesh=mesh,
        in_specs=(P(("dp", "cent"), None), P("cent", None)),
        out_specs=P("dp", "cent"),
        check_vma=False,
    )
```

```python
import functools
import math

import jax
import jax.numpy as jnp
from jax import lax
from jax.experimental import pallas as pl
from jax.experimental.pallas import tpu as pltpu
from jax.sharding import PartitionSpec as P

BETA_GAIN = 4.0
PRIOR = 0.5
MESH = pl.DeviceIdType.MESH
NT = (((1,), (1,)), ((), ()))


def general(points, centroids):
    features = points.shape[1]
    sharpness = BETA_GAIN * features ** (-0.5)
    gathered = lax.all_gather(points, "cent", axis=0, tiled=True)
    sqnorm = jnp.sum(jnp.square(centroids.astype(jnp.float32)), axis=1)
    total_rows = gathered.shape[0]
    block_rows = min(512, total_rows)
    blocks = gathered.reshape(total_rows // block_rows, block_rows, features)
    shard_cents = centroids.shape[0]

    def logits_of(xblock):
        dots = lax.dot_general(xblock, centroids, NT, preferred_element_type=jnp.float32)
        return sharpness * (dots - 0.5 * sqnorm[None, :])

    def resp_of(logits, row_top, row_total):
        return (jnp.exp(logits - row_top[:, None]) / row_total[:, None]).astype(jnp.bfloat16)

    logits = lax.map(logits_of, blocks)
    local_max = jnp.max(logits, axis=-1)
    local_sum = jnp.sum(jnp.exp(logits - local_max[..., None]), axis=-1)
    row_top = lax.pmax(local_max, "cent")
    row_total = lax.psum(local_sum * jnp.exp(local_max - row_top), "cent")
    resp = jax.vmap(resp_of)(logits, row_top, row_total)
    resp = resp.reshape(total_rows, shard_cents)
    counts = jnp.sum(resp.astype(jnp.float32), axis=0)
    dp_count = lax.axis_size("dp")
    dp_index = lax.axis_index("dp")
    column_share = features // dp_count
    numer = lax.psum_scatter(
        lax.dot_general(
            gathered, resp, (((0,), (0,)), ((), ())), preferred_element_type=jnp.float32
        ).astype(jnp.bfloat16),
        "dp",
        scatter_dimension=0,
        tiled=True,
    ).astype(jnp.float32)
    counts_all = lax.psum(counts, "dp")
    own_cols = (
        lax.dynamic_slice_in_dim(centroids, dp_index * column_share, column_share, 1)
        .astype(jnp.float32)
        .T
    )
    return (numer + PRIOR * own_cols) / (counts_all[None, :] + PRIOR)


NZ = 4
NC = 8
PIECE = 512
CHUNK = 1024


ORDER = (
    "c0", "x0", "y0", "c1", "x1", "c2", "y1", "d0",
    "x2", "c3", "y2", "x3", "d1", "y3", "d2", "d3",
)
DIGITS = tuple(
    tuple(
        sum(f(b) << (2 * i) for i, b in enumerate(ORDER[h:h + 8])) for h in (0, 8)
    )
    for f in (lambda b: int(b[1]), lambda b: int(b[0] in "xd"), lambda b: int(b[0] in "yd"))
)


def order_digit(k, n):
    return (jnp.where(n < 8, DIGITS[k][0], DIGITS[k][1]) >> (2 * (n % 8))) % 4


def fused(
    points_ref, cents_ref, out_ref,
    x_ref, c_ref, far_ref, e_ref, a0_ref, a1_ref, bias_ref, buf0, buf1, buf2, obuf,
    mstat, scale_ref, scale_t, gath, lone, nsend, nrecv, csend, crecv,
    load_sem, send_sem, recv_sem, stat_send, stat_recv, pair_send, pair_recv, out_sem,
):
    shard, feats = points_ref.shape
    n_chunk = cents_ref.shape[0] // CHUNK - 1
    kc = n_chunk * CHUNK
    block = 2 * shard
    group = NC * shard
    own_feats = feats // NZ
    gain = BETA_GAIN * feats ** (-0.5) * math.log2(math.e)

    z = lax.axis_index("dp")
    cent = lax.axis_index("cent")
    core = cent % 2
    xx = (cent // 2) % 2
    yy = cent // 4
    flip = z // 2
    odd = z % 2
    pz = z + 1 - 2 * odd
    lone_row = pl.multiple_of(odd * kc, CHUNK)
    far_row = pl.multiple_of((1 - odd) * kc, CHUNK)
    zz = z + flip * (3 - 2 * z)

    def z_of(j):
        s = (1 - zz) if j == 1 else (zz if j == 0 else j)
        return s + flip * (3 - 2 * s)

    def pos_of(pos):
        fx = pos in ("x", "d")
        fy = pos in ("y", "d")
        return ((1 - yy) if fy else yy) * 2 + ((1 - xx) if fx else xx)

    x_peer = (z, (yy * 2 + 1 - xx) * 2 + core)
    y_peer = (z, ((1 - yy) * 2 + xx) * 2 + core)
    sib = (z, cent + 1 - 2 * core)

    def piece(sid):
        return x_ref.at[pl.ds(pl.multiple_of(sid * shard, shard), shard)]

    def sid_of(j, pos, other=False):
        return z_of(j) * NC + pos_of(pos) * 2 + ((1 - core) if other else core)

    def copy_to(sid, dev, slot):
        return pltpu.make_async_remote_copy(
            src_ref=piece(sid), dst_ref=piece(sid), send_sem=send_sem.at[slot],
            recv_sem=recv_sem.at[sid], device_id=dev, device_id_type=MESH,
        )

    def wait_piece(sid):
        copy_to(sid, sib, 0).wait_recv()

    POS = {"c": 0, "x": 1, "y": 2, "d": 3}

    def routes(j, pos):
        base = (j * 4 + POS[pos]) * 5
        r = []
        if pos == "c":
            zj = z_of(j)
            up = (zj <= z) & (z < NZ - 1)
            down = (zj >= z) & (z > 0)
            r.append((up, (z + 1, cent), base))
            r.append((down, (z - 1, cent), base + 1))
            r.append((None, x_peer, base + 2))
            r.append((None, y_peer, base + 3))
        if pos == "x" and j % 2 == 0:
            r.append((None, y_peer, base + 3))
        if pos == "y" and j % 2 == 1:
            r.append((None, x_peer, base + 2))
        r.append((None, sib, base + 4))
        return r

    def each_route(j, pos, act):
        sid = sid_of(j, pos)
        for cond, dev, slot in routes(j, pos):
            if cond is None:
                act(copy_to(sid, dev, slot))
            else:
                @pl.when(cond)
                def _(dev=dev, slot=slot):
                    act(copy_to(sid, dev, slot))

    def pass_on(j, pos):
        if (j, pos) != (0, "c"):
            wait_piece(sid_of(j, pos))
        each_route(j, pos, lambda c: c.start())

    own_id = sid_of(0, "c")
    load_x = pltpu.make_async_copy(points_ref, piece(own_id), load_sem.at[0])
    own_col = pl.ds(pl.multiple_of(z * own_feats, own_feats), own_feats)
    pair_col = pl.ds(pl.multiple_of(pz * own_feats, own_feats), own_feats)
    loads = [
        pltpu.make_async_copy(
            cents_ref.at[pl.ds(lone_row, CHUNK)], c_ref.at[pl.ds(0, CHUNK)], load_sem.at[1]
        ),
        pltpu.make_async_copy(
            cents_ref.at[pl.ds(CHUNK, kc - CHUNK)], c_ref.at[pl.ds(CHUNK, kc - CHUNK)],
            load_sem.at[2],
        ),
        pltpu.make_async_copy(
            cents_ref.at[pl.ds(far_row, CHUNK), own_col], far_ref, load_sem.at[3]
        ),
    ]
    load_x.start()
    for c in loads:
        c.start()
    barrier = pltpu.get_barrier_semaphore()
    for d in range(1, NC):
        pl.semaphore_signal(barrier, inc=1, device_id=(z, (cent + d) % NC), device_id_type=MESH)
    for d in range(NC):
        pl.semaphore_signal(barrier, inc=1, device_id=(pz, (cent + d) % NC), device_id_type=MESH)
    inner_z = jnp.minimum(z, 1) * jnp.minimum(NZ - 1 - z, 1)

    @pl.when(inner_z == 1)
    def _():
        pl.semaphore_signal(barrier, inc=1, device_id=(3 - z, cent), device_id_type=MESH)

    pl.semaphore_wait(barrier, 2 * NC - 1 + inner_z)

    load_x.wait()
    pass_on(0, "c")
    for c in loads:
        c.wait()

    def norm_step(r, _):
        rows = pl.ds(pl.multiple_of(r * 256, 256), 256)
        v = c_ref[rows, :].astype(jnp.float32)
        s = jnp.sum(v * v, axis=1, keepdims=True) * 0.5
        bias_ref[rows, :] = jnp.broadcast_to(s, (256, 128))
        return 0

    lax.fori_loop(0, kc // 256, norm_step, 0)

    def stat_copy(j, d):
        zj = z_of(j)
        if d < NC:
            src, slot, dev = gath.at[cent, zj], cent, (z, (cent + d) % NC)
        else:
            src, slot, dev = lone.at[zj], cent + NC, (pz, (cent + d) % NC)
        return pltpu.make_async_remote_copy(
            src_ref=src, dst_ref=gath.at[slot, zj],
            send_sem=stat_send.at[j, d], recv_sem=stat_recv.at[slot, zj],
            device_id=dev, device_id_type=MESH,
        )

    bufs = (buf0, buf1, buf2)
    n_piece = CHUNK // PIECE
    end = 1 - inner_z

    def top8(v):
        return jnp.max(v.reshape(v.shape[0] // 8, 8, v.shape[1]), axis=0)

    def dots(c, p, xb):
        ks = slice(c * CHUNK + p * PIECE, c * CHUNK + (p + 1) * PIECE)
        v = lax.dot_general(c_ref[ks, :], xb, NT, preferred_element_type=jnp.float32)
        b = bias_ref[ks, :]
        v = v - jnp.concatenate([b] * (block // 128), axis=1)
        bufs[c][p * PIECE:(p + 1) * PIECE, :] = v
        return top8(v)

    def expo(c, p, m, rows):
        v = bufs[c][p * PIECE:(p + 1) * PIECE, :]
        e = jnp.exp2((v - m) * gain)
        e_ref[c * CHUNK + p * PIECE:c * CHUNK + (p + 1) * PIECE, rows] = e.astype(jnp.bfloat16)
        return jnp.sum(e.reshape(PIECE // 8, 8, block), axis=0)

    def finish(zj, pid, tops, sums):
        rows = pl.ds(pl.multiple_of(zj * group + pid * block, block), block)
        for c in range(n_chunk):
            mstat[c:c + 1, rows] = tops[c]
        top = functools.reduce(jnp.maximum, tops)
        total = sum(l * jnp.exp2((m - top) * gain) for m, l in zip(tops, sums))
        inner = pl.ds(pl.multiple_of(pid * block, block), block)
        gath[cent, zj, 0:1, inner] = top
        gath[cent, zj, 1:2, inner] = total
        lone[zj, 0:1, inner] = tops[0]
        lone[zj, 1:2, inner] = sums[0]

    def row_max(parts):
        return jnp.max(functools.reduce(jnp.maximum, parts), axis=0, keepdims=True)

    def row_sum(parts):
        return jnp.sum(sum(parts), axis=0, keepdims=True)

    def send_stats(j):
        for d in range(1, 2 * NC):
            stat_copy(j, d).start()

    def step(n, carry):
        pzj, ppid, ptops, psums = carry
        for at, items in (
            (1, ((0, "x"), (0, "y"), (1, "c"))),
            (1 + 2 * end, ((2, "c"),)),
            (3, ((1, "x"),)),
            (3 + 2 * end, ((3, "c"),)),
            (5, ((1, "y"), (0, "d"), (2, "x"))),
            (7, ((2, "y"),)),
            (9, ((3, "x"), (1, "d"))),
            (11, ((3, "y"), (2, "d"))),
            (14, ((3, "d"),)),
        ):
            @pl.when(n == at)
            def _(items=items):
                for j, pos in items:
                    pass_on(j, pos)

        j, fx, fy = (order_digit(k, n) for k in range(3))
        j1 = jnp.where(j == 1, 1, 0)
        j0 = jnp.where(j == 0, 1, 0)
        s = j0 * zz + j1 * (1 - zz) + (1 - j0 - j1) * j
        zj = s + flip * (3 - 2 * s)
        py = yy + fy * (1 - 2 * yy)
        px = xx + fx * (1 - 2 * xx)
        pid = py * 2 + px
        wait_piece(zj * NC + pid * 2 + 1 - core)
        rows = pl.ds(pl.multiple_of(zj * group + pid * block, block), block)
        prows = pl.ds(pl.multiple_of(pzj * group + ppid * block, block), block)
        xb = x_ref[rows, :]

        tops, sums = [], []
        m, where = ptops[-1], prows
        for c in range(n_chunk):
            t8, s8 = [], []
            for p in range(n_piece):
                t8.append(dots(c, p, xb))
                s8.append(expo((c - 1) % n_chunk, p, m, where))
            if c == 0:
                finish(pzj, ppid, ptops, list(psums) + [row_sum(s8)])
            else:
                sums.append(row_sum(s8))
            m, where = row_max(t8), rows
            tops.append(m)

        for at, jj in ((8, 0), (13, 1), (15, 2)):
            @pl.when(n == at)
            def _(jj=jj):
                send_stats(jj)
        return zj, pid, tuple(tops), tuple(sums)

    last_buf = bufs[n_chunk - 1]
    last_buf[...] = jnp.zeros_like(last_buf)
    zero = jnp.zeros((1, block), jnp.float32)
    pzj, ppid, ptops, psums = lax.fori_loop(
        0, 16, step, (z, yy * 2 + xx, (zero,) * n_chunk, (zero,) * (n_chunk - 1))
    )
    prows = pl.ds(pl.multiple_of(pzj * group + ppid * block, block), block)
    s8 = [expo(n_chunk - 1, p, ptops[-1], prows) for p in range(n_piece)]
    finish(pzj, ppid, ptops, list(psums) + [row_sum(s8)])
    send_stats(3)

    for d in range(1, 2 * NC):
        frm = (cent + d) % NC + (NC if d >= NC else 0)
        for w in range(NZ):
            pltpu.make_async_remote_copy(
                src_ref=gath.at[frm, w], dst_ref=gath.at[frm, w],
                send_sem=stat_send.at[0, 0], recv_sem=stat_recv.at[frm, w],
                device_id=sib, device_id_type=MESH,
            ).wait_recv()
    scale_ref[...] = jnp.zeros_like(scale_ref)
    for w in range(NZ):
        cols = slice(w * group, (w + 1) * group)
        ms = [gath[q, w, 0:1, :] for q in range(2 * NC)]
        top = functools.reduce(jnp.maximum, ms)
        total = sum(
            gath[q, w, 1:2, :] * jnp.exp2((ms[q] - top) * gain) for q in range(2 * NC)
        )
        inv = 1.0 / total
        for c in range(n_chunk):
            scale_ref[c:c + 1, cols] = jnp.exp2((mstat[c:c + 1, cols] - top) * gain) * inv

    sub = obuf.shape[2]
    n_sub = CHUNK // sub
    slots = obuf.shape[0]
    a_refs = (a0_ref, a1_ref)
    writes = []

    def write(value, row):
        t = len(writes)
        if t >= slots:
            writes[t - slots].wait()
        obuf[t % slots] = value
        copy = pltpu.make_async_copy(
            obuf.at[t % slots], out_ref.at[:, pl.ds(row, sub)], out_sem.at[t % slots]
        )
        copy.start()
        writes.append(copy)

    def pair_copies(u):
        return [
            pltpu.make_async_remote_copy(
                src_ref=src.at[u], dst_ref=dst.at[u], send_sem=pair_send.at[i, u],
                recv_sem=pair_recv.at[i, u], device_id=(pz, cent), device_id_type=MESH,
            )
            for i, (src, dst) in enumerate(((nsend, nrecv), (csend, crecv)))
        ]

    scale_t[...] = scale_ref[...].T

    def prepare(c):
        for half, cols in enumerate((own_col, pair_col) if c == 0 else (own_col,)):
            scaled = x_ref[:, cols].astype(jnp.float32) * scale_t[:, c:c + 1]
            a_refs[c % 2][:, half * own_feats:(half + 1) * own_feats] = scaled.astype(jnp.bfloat16)

    def multiply(c, u):
        width = own_feats * (2 if c == 0 else 1)
        ks = slice(c * CHUNK + u * sub, c * CHUNK + (u + 1) * sub)
        res = jnp.dot(
            e_ref[ks, :], a_refs[c % 2][:, 0:width], preferred_element_type=jnp.float32
        )
        parts = []
        for r in range(ks.start, ks.stop, 128):
            acc = jnp.zeros((128, 128), jnp.float32)
            for i in range(0, e_ref.shape[1], 128):
                e = e_ref[r:r + 128, i:i + 128].astype(jnp.float32)
                acc = acc + e * scale_ref[c:c + 1, i:i + 128]
            parts.append(jnp.sum(acc, axis=1, keepdims=True))
        counts = jnp.concatenate(parts, axis=0)
        counts = jnp.broadcast_to(counts, (sub, 128)).T[0:8]
        if c == 0:
            nsend[u] = res[:, own_feats:].T.astype(jnp.bfloat16)
            csend[u] = counts
            for copy in pair_copies(u):
                copy.start()
        return res[:, :own_feats].T, counts[0:1]

    def conclude(c, u, numer, counts):
        ks = slice(c * CHUNK + u * sub, c * CHUNK + (u + 1) * sub)
        own = c_ref[ks, own_col].astype(jnp.float32).T
        base = lone_row if c == 0 else c * CHUNK
        write((numer + PRIOR * own) * (1.0 / (counts + PRIOR)), base + u * sub)

    prepare(0)
    pending = None
    for c in range(n_chunk):
        for u in range(n_sub):
            done = multiply(c, u)
            if u == 0 and c + 1 < n_chunk:
                prepare(c + 1)
            if pending is not None:
                conclude(*pending)
            pending = (c, u, *done)
    conclude(*pending)
    for u in range(n_sub):
        for copy in pair_copies(u):
            copy.wait_recv()
        own = far_ref[u * sub:(u + 1) * sub, :].astype(jnp.float32).T
        counts = crecv[u][0:1]
        write(
            (nrecv[u].astype(jnp.float32) + PRIOR * own) * (1.0 / (counts + PRIOR)),
            pl.multiple_of(far_row + u * sub, sub),
        )
    for copy in writes[-slots:]:
        copy.wait()
    for u in range(n_sub):
        for copy in pair_copies(u):
            copy.wait_send()
    for j in range(NZ):
        for pos in POS:
            each_route(j, pos, lambda c: c.wait_send())
        for d in range(1, 2 * NC):
            stat_copy(j, d).wait_send()


def fused_local(points, centroids):
    shard, feats = points.shape
    all_kc = centroids.shape[0]
    kc = all_kc - CHUNK
    half = CHUNK // 2
    rows = shard * NZ * NC
    own = feats // NZ
    dma = pltpu.SemaphoreType.DMA
    return pl.pallas_call(
        fused,
        out_shape=jax.ShapeDtypeStruct((own, all_kc), jnp.float32),
        in_specs=[pl.BlockSpec(memory_space=pl.ANY)] * 2,
        out_specs=pl.BlockSpec(memory_space=pl.ANY),
        scratch_shapes=[
            pltpu.VMEM((rows, feats), jnp.bfloat16),
            pltpu.VMEM((kc, feats), jnp.bfloat16),
            pltpu.VMEM((CHUNK, own), jnp.bfloat16),
            pltpu.VMEM((kc, rows), jnp.bfloat16),
            pltpu.VMEM((rows, 2 * own), jnp.bfloat16),
            pltpu.VMEM((rows, own), jnp.bfloat16),
            pltpu.VMEM((kc, 128), jnp.float32),
            pltpu.VMEM((CHUNK, 2 * shard), jnp.float32),
            pltpu.VMEM((CHUNK, 2 * shard), jnp.float32),
            pltpu.VMEM((CHUNK, 2 * shard), jnp.float32),
            pltpu.VMEM((4, own, half), jnp.float32),
            pltpu.VMEM((kc // CHUNK, rows), jnp.float32),
            pltpu.VMEM((8, rows), jnp.float32),
            pltpu.VMEM((rows, 8), jnp.float32),
            pltpu.VMEM((2 * NC, NZ, 2, NC * shard), jnp.float32),
            pltpu.VMEM((NZ, 2, NC * shard), jnp.float32),
            pltpu.VMEM((2, own, half), jnp.bfloat16),
            pltpu.VMEM((2, own, half), jnp.bfloat16),
            pltpu.VMEM((2, 8, half), jnp.float32),
            pltpu.VMEM((2, 8, half), jnp.float32),
            dma((4,)),
            dma((NZ * 4 * 5,)),
            dma((NZ * NC,)),
            dma((NZ, 2 * NC)),
            dma((2 * NC, NZ)),
            dma((2, 2)),
            dma((2, 2)),
            dma((4,)),
        ],
        compiler_params=pltpu.CompilerParams(
            collective_id=0, has_side_effects=True, vmem_limit_bytes=62 * 2**20
        ),
        cost_estimate=pl.CostEstimate(
            flops=2 * rows * kc * (feats + own), bytes_accessed=2 * kc * feats + 4 * own * kc,
            transcendentals=rows * kc,
        ),
    )(points, centroids)


def solution(mesh):
    def local(points, centroids):
        small = (
            mesh.shape["dp"] == NZ and mesh.shape["cent"] == NC
            and points.shape == (128, 1024) and centroids.shape == (4096, 1024)
        )
        return fused_local(points, centroids) if small else general(points, centroids)

    return jax.shard_map(
        local,
        mesh=mesh,
        in_specs=(P(("dp", "cent"), None), P("cent", None)),
        out_specs=P("dp", "cent"),
        check_vma=False,
    )
```

```python
import functools
import math

import jax
import jax.numpy as jnp
from jax import lax
from jax.experimental import pallas as pl
from jax.experimental.pallas import tpu as pltpu
from jax.sharding import PartitionSpec as P

BETA_GAIN = 4.0
PRIOR = 0.5
MESH = pl.DeviceIdType.MESH
NT = (((1,), (1,)), ((), ()))


def general(points, centroids):
    features = points.shape[1]
    sharpness = BETA_GAIN * features ** (-0.5)
    gathered = lax.all_gather(points, "cent", axis=0, tiled=True)
    sqnorm = jnp.sum(jnp.square(centroids.astype(jnp.float32)), axis=1)
    total_rows = gathered.shape[0]
    block_rows = min(512, total_rows)
    blocks = gathered.reshape(total_rows // block_rows, block_rows, features)
    shard_cents = centroids.shape[0]

    def logits_of(xblock):
        dots = lax.dot_general(xblock, centroids, NT, preferred_element_type=jnp.float32)
        return sharpness * (dots - 0.5 * sqnorm[None, :])

    def resp_of(logits, row_top, row_total):
        return (jnp.exp(logits - row_top[:, None]) / row_total[:, None]).astype(jnp.bfloat16)

    logits = lax.map(logits_of, blocks)
    local_max = jnp.max(logits, axis=-1)
    local_sum = jnp.sum(jnp.exp(logits - local_max[..., None]), axis=-1)
    row_top = lax.pmax(local_max, "cent")
    row_total = lax.psum(local_sum * jnp.exp(local_max - row_top), "cent")
    resp = jax.vmap(resp_of)(logits, row_top, row_total)
    resp = resp.reshape(total_rows, shard_cents)
    counts = jnp.sum(resp.astype(jnp.float32), axis=0)
    dp_count = lax.axis_size("dp")
    dp_index = lax.axis_index("dp")
    column_share = features // dp_count
    numer = lax.psum_scatter(
        lax.dot_general(
            gathered, resp, (((0,), (0,)), ((), ())), preferred_element_type=jnp.float32
        ).astype(jnp.bfloat16),
        "dp",
        scatter_dimension=0,
        tiled=True,
    ).astype(jnp.float32)
    counts_all = lax.psum(counts, "dp")
    own_cols = (
        lax.dynamic_slice_in_dim(centroids, dp_index * column_share, column_share, 1)
        .astype(jnp.float32)
        .T
    )
    return (numer + PRIOR * own_cols) / (counts_all[None, :] + PRIOR)


NZ = 4
NC = 8
PIECE = 512
CHUNK = 1024


ORDER = (
    "c0", "x0", "y0", "c1", "x1", "c2", "y1", "d0",
    "x2", "c3", "y2", "x3", "d1", "y3", "d2", "d3",
)
DIGITS = tuple(
    tuple(
        sum(f(b) << (2 * i) for i, b in enumerate(ORDER[h:h + 8])) for h in (0, 8)
    )
    for f in (lambda b: int(b[1]), lambda b: int(b[0] in "xd"), lambda b: int(b[0] in "yd"))
)


def order_digit(k, n):
    return (jnp.where(n < 8, DIGITS[k][0], DIGITS[k][1]) >> (2 * (n % 8))) % 4


def fused(
    points_ref, cents_ref, out_ref,
    x_ref, c_ref, e_ref, xt_ref, a_ref, bias_ref, buf0, buf1, obuf, mstat, scale_ref, gath,
    load_sem, send_sem, recv_sem, stat_send, stat_recv, out_sem,
):
    shard, feats = points_ref.shape
    kc = cents_ref.shape[0]
    n_chunk = kc // CHUNK
    block = 2 * shard
    group = NC * shard
    own_feats = feats // NZ
    gain = BETA_GAIN * feats ** (-0.5) * math.log2(math.e)

    z = lax.axis_index("dp")
    cent = lax.axis_index("cent")
    core = cent % 2
    xx = (cent // 2) % 2
    yy = cent // 4
    flip = z // 2
    zz = z + flip * (3 - 2 * z)

    def z_of(j):
        s = (1 - zz) if j == 1 else (zz if j == 0 else j)
        return s + flip * (3 - 2 * s)

    def pos_of(pos):
        fx = pos in ("x", "d")
        fy = pos in ("y", "d")
        return ((1 - yy) if fy else yy) * 2 + ((1 - xx) if fx else xx)

    x_peer = (z, (yy * 2 + 1 - xx) * 2 + core)
    y_peer = (z, ((1 - yy) * 2 + xx) * 2 + core)
    sib = (z, cent + 1 - 2 * core)

    def piece(sid):
        return x_ref.at[pl.ds(pl.multiple_of(sid * shard, shard), shard)]

    def sid_of(j, pos, other=False):
        return z_of(j) * NC + pos_of(pos) * 2 + ((1 - core) if other else core)

    def copy_to(sid, dev, slot):
        return pltpu.make_async_remote_copy(
            src_ref=piece(sid), dst_ref=piece(sid), send_sem=send_sem.at[slot],
            recv_sem=recv_sem.at[sid], device_id=dev, device_id_type=MESH,
        )

    def wait_piece(sid):
        copy_to(sid, sib, 0).wait_recv()

    POS = {"c": 0, "x": 1, "y": 2, "d": 3}

    def routes(j, pos):
        base = (j * 4 + POS[pos]) * 5
        r = []
        if pos == "c":
            zj = z_of(j)
            up = (zj <= z) & (z < NZ - 1)
            down = (zj >= z) & (z > 0)
            r.append((up, (z + 1, cent), base))
            r.append((down, (z - 1, cent), base + 1))
            r.append((None, x_peer, base + 2))
            r.append((None, y_peer, base + 3))
        if pos == "x" and j % 2 == 0:
            r.append((None, y_peer, base + 3))
        if pos == "y" and j % 2 == 1:
            r.append((None, x_peer, base + 2))
        r.append((None, sib, base + 4))
        return r

    def each_route(j, pos, act):
        sid = sid_of(j, pos)
        for cond, dev, slot in routes(j, pos):
            if cond is None:
                act(copy_to(sid, dev, slot))
            else:
                @pl.when(cond)
                def _(dev=dev, slot=slot):
                    act(copy_to(sid, dev, slot))

    def pass_on(j, pos):
        if (j, pos) != (0, "c"):
            wait_piece(sid_of(j, pos))
        each_route(j, pos, lambda c: c.start())

    own_id = sid_of(0, "c")
    load_x = pltpu.make_async_copy(points_ref, piece(own_id), load_sem.at[0])
    load_c = pltpu.make_async_copy(cents_ref, c_ref, load_sem.at[1])
    load_x.start()
    load_c.start()
    barrier = pltpu.get_barrier_semaphore()
    for d in range(1, NC):
        pl.semaphore_signal(barrier, inc=1, device_id=(z, (cent + d) % NC), device_id_type=MESH)

    @pl.when(z > 0)
    def _():
        pl.semaphore_signal(barrier, inc=1, device_id=(z - 1, cent), device_id_type=MESH)

    @pl.when(z < NZ - 1)
    def _():
        pl.semaphore_signal(barrier, inc=1, device_id=(z + 1, cent), device_id_type=MESH)

    inner_z = jnp.minimum(z, 1) * jnp.minimum(NZ - 1 - z, 1)
    pl.semaphore_wait(barrier, NC + inner_z)

    load_x.wait()
    pass_on(0, "c")
    load_c.wait()

    def norm_step(r, _):
        rows = pl.ds(pl.multiple_of(r * 256, 256), 256)
        v = c_ref[rows, :].astype(jnp.float32)
        s = jnp.sum(v * v, axis=1, keepdims=True) * 0.5
        bias_ref[rows, :] = jnp.broadcast_to(s, (256, 128))
        return 0

    lax.fori_loop(0, kc // 256, norm_step, 0)

    def stat_copy(j, d):
        zj = z_of(j)
        return pltpu.make_async_remote_copy(
            src_ref=gath.at[cent, zj], dst_ref=gath.at[cent, zj],
            send_sem=stat_send.at[j, d], recv_sem=stat_recv.at[cent, zj],
            device_id=(z, (cent + d) % NC), device_id_type=MESH,
        )

    own_col = pl.ds(pl.multiple_of(z * own_feats, own_feats), own_feats)
    bufs = (buf0, buf1)
    n_piece = CHUNK // PIECE
    end = 1 - jnp.minimum(z, 1) * jnp.minimum(NZ - 1 - z, 1)

    def top8(v):
        return jnp.max(v.reshape(v.shape[0] // 8, 8, v.shape[1]), axis=0)

    def dots(c, p, xb):
        ks = slice(c * CHUNK + p * PIECE, c * CHUNK + (p + 1) * PIECE)
        v = lax.dot_general(c_ref[ks, :], xb, NT, preferred_element_type=jnp.float32)
        b = bias_ref[ks, :]
        v = v - jnp.concatenate([b] * (block // 128), axis=1)
        bufs[c % 2][p * PIECE:(p + 1) * PIECE, :] = v
        return top8(v)

    def expo(c, p, m, rows):
        v = bufs[c % 2][p * PIECE:(p + 1) * PIECE, :]
        e = jnp.exp2((v - m) * gain)
        e_ref[c * CHUNK + p * PIECE:c * CHUNK + (p + 1) * PIECE, rows] = e.astype(jnp.bfloat16)
        return jnp.sum(e.reshape(PIECE // 8, 8, block), axis=0)

    def finish(zj, pid, tops, sums):
        rows = pl.ds(pl.multiple_of(zj * group + pid * block, block), block)
        for c in range(n_chunk):
            mstat[c:c + 1, rows] = tops[c]
        top = functools.reduce(jnp.maximum, tops)
        total = sum(l * jnp.exp2((m - top) * gain) for m, l in zip(tops, sums))
        inner = pl.ds(pl.multiple_of(pid * block, block), block)
        gath[cent, zj, 0:1, inner] = top
        gath[cent, zj, 1:2, inner] = total

    def row_max(parts):
        return jnp.max(functools.reduce(jnp.maximum, parts), axis=0, keepdims=True)

    def row_sum(parts):
        return jnp.sum(sum(parts), axis=0, keepdims=True)

    def send_stats(j):
        for d in range(1, NC):
            stat_copy(j, d).start()

    def step(n, carry):
        pzj, ppid, ptops, psums = carry
        for at, items in (
            (1, ((0, "x"), (0, "y"), (1, "c"))),
            (1 + 2 * end, ((2, "c"),)),
            (3, ((1, "x"),)),
            (3 + 2 * end, ((3, "c"),)),
            (5, ((1, "y"), (0, "d"), (2, "x"))),
            (7, ((2, "y"),)),
            (9, ((3, "x"), (1, "d"))),
            (11, ((3, "y"), (2, "d"))),
            (14, ((3, "d"),)),
        ):
            @pl.when(n == at)
            def _(items=items):
                for j, pos in items:
                    pass_on(j, pos)

        j, fx, fy = (order_digit(k, n) for k in range(3))
        j1 = jnp.where(j == 1, 1, 0)
        j0 = jnp.where(j == 0, 1, 0)
        s = j0 * zz + j1 * (1 - zz) + (1 - j0 - j1) * j
        zj = s + flip * (3 - 2 * s)
        py = yy + fy * (1 - 2 * yy)
        px = xx + fx * (1 - 2 * xx)
        pid = py * 2 + px
        wait_piece(zj * NC + pid * 2 + 1 - core)
        rows = pl.ds(pl.multiple_of(zj * group + pid * block, block), block)
        prows = pl.ds(pl.multiple_of(pzj * group + ppid * block, block), block)
        xb = x_ref[rows, :]

        tops, sums = [], []
        m, where = ptops[-1], prows
        for c in range(n_chunk):
            t8, s8 = [], []
            for p in range(n_piece):
                t8.append(dots(c, p, xb))
                s8.append(expo((c - 1) % n_chunk, p, m, where))
            if c == 0:
                finish(pzj, ppid, ptops, list(psums) + [row_sum(s8)])
                xt_ref[:, rows] = x_ref[rows, own_col].astype(jnp.float32).T.astype(jnp.bfloat16)
            else:
                sums.append(row_sum(s8))
            m, where = row_max(t8), rows
            tops.append(m)

        for at, jj in ((8, 0), (13, 1), (15, 2)):
            @pl.when(n == at)
            def _(jj=jj):
                send_stats(jj)
        return zj, pid, tuple(tops), tuple(sums)

    last_buf = bufs[(n_chunk - 1) % 2]
    last_buf[...] = jnp.zeros_like(last_buf)
    zero = jnp.zeros((1, block), jnp.float32)
    pzj, ppid, ptops, psums = lax.fori_loop(
        0, 16, step, (z, yy * 2 + xx, (zero,) * n_chunk, (zero,) * (n_chunk - 1))
    )
    prows = pl.ds(pl.multiple_of(pzj * group + ppid * block, block), block)
    s8 = [expo(n_chunk - 1, p, ptops[-1], prows) for p in range(n_piece)]
    finish(pzj, ppid, ptops, list(psums) + [row_sum(s8)])
    send_stats(3)

    for d in range(1, NC):
        frm = (cent + d) % NC
        for w in range(NZ):
            pltpu.make_async_remote_copy(
                src_ref=gath.at[frm, w], dst_ref=gath.at[frm, w],
                send_sem=stat_send.at[0, 0], recv_sem=stat_recv.at[frm, w],
                device_id=sib, device_id_type=MESH,
            ).wait_recv()
    for w in range(NZ):
        cols = slice(w * group, (w + 1) * group)
        ms = [gath[q, w, 0:1, :] for q in range(NC)]
        top = functools.reduce(jnp.maximum, ms)
        total = sum(gath[q, w, 1:2, :] * jnp.exp2((ms[q] - top) * gain) for q in range(NC))
        inv = 1.0 / total
        for c in range(n_chunk):
            scale_ref[c:c + 1, cols] = jnp.exp2((mstat[c:c + 1, cols] - top) * gain) * inv

    sub = obuf.shape[2]
    n_sub = CHUNK // sub
    slots = obuf.shape[0]
    writes = []

    def prepare(c):
        sc = scale_ref[c:c + 1, :]
        a = a_ref
        a[0:own_feats, :] = (xt_ref[...].astype(jnp.float32) * sc).astype(jnp.bfloat16)
        hi = sc.astype(jnp.bfloat16).astype(jnp.float32)
        which = lax.broadcasted_iota(jnp.int32, (16, sc.shape[1]), 0)
        extra = jnp.where(which == 0, hi, jnp.where(which == 1, sc - hi, 0.0))
        a[own_feats:own_feats + 16, :] = extra.astype(jnp.bfloat16)

    def multiply(c, u):
        ks = slice(c * CHUNK + u * sub, c * CHUNK + (u + 1) * sub)
        return lax.dot_general(
            a_ref[...], e_ref[ks, :], NT, preferred_element_type=jnp.float32
        )

    def conclude(c, u, res):
        ks = slice(c * CHUNK + u * sub, c * CHUNK + (u + 1) * sub)
        counts = res[own_feats:own_feats + 1] + res[own_feats + 1:own_feats + 2]
        own = c_ref[ks, own_col].astype(jnp.float32).T
        t = len(writes)
        if t >= slots:
            writes[t - slots].wait()
        obuf[t % slots] = (res[:own_feats] + PRIOR * own) * (1.0 / (counts + PRIOR))
        copy = pltpu.make_async_copy(obuf.at[t % slots], out_ref.at[:, ks], out_sem.at[t % slots])
        copy.start()
        writes.append(copy)

    pending = None
    for c in range(n_chunk):
        prepare(c)
        for u in range(n_sub):
            res = multiply(c, u)
            if pending is not None:
                conclude(*pending)
            pending = (c, u, res)
    conclude(*pending)
    for copy in writes[-slots:]:
        copy.wait()
    for j in range(NZ):
        for pos in POS:
            each_route(j, pos, lambda c: c.wait_send())
        for d in range(1, NC):
            stat_copy(j, d).wait_send()


def fused_local(points, centroids):
    shard, feats = points.shape
    kc = centroids.shape[0]
    rows = shard * NZ * NC
    own = feats // NZ
    dma = pltpu.SemaphoreType.DMA
    return pl.pallas_call(
        fused,
        out_shape=jax.ShapeDtypeStruct((own, kc), jnp.float32),
        in_specs=[pl.BlockSpec(memory_space=pl.ANY)] * 2,
        out_specs=pl.BlockSpec(memory_space=pl.ANY),
        scratch_shapes=[
            pltpu.VMEM((rows, feats), jnp.bfloat16),
            pltpu.VMEM((kc, feats), jnp.bfloat16),
            pltpu.VMEM((kc, rows), jnp.bfloat16),
            pltpu.VMEM((own, rows), jnp.bfloat16),
            pltpu.VMEM((own + 16, rows), jnp.bfloat16),
            pltpu.VMEM((kc, 128), jnp.float32),
            pltpu.VMEM((CHUNK, 2 * shard), jnp.float32),
            pltpu.VMEM((CHUNK, 2 * shard), jnp.float32),
            pltpu.VMEM((2, own, CHUNK // 2), jnp.float32),
            pltpu.VMEM((kc // CHUNK, rows), jnp.float32),
            pltpu.VMEM((kc // CHUNK, rows), jnp.float32),
            pltpu.VMEM((NC, NZ, 2, NC * shard), jnp.float32),
            dma((2,)),
            dma((NZ * 4 * 5,)),
            dma((NZ * NC,)),
            dma((NZ, NC)),
            dma((NC, NZ)),
            dma((2,)),
        ],
        compiler_params=pltpu.CompilerParams(
            collective_id=0, has_side_effects=True, vmem_limit_bytes=62 * 2**20
        ),
        cost_estimate=pl.CostEstimate(
            flops=2 * rows * kc * (feats + own), bytes_accessed=2 * kc * feats + 4 * own * kc,
            transcendentals=rows * kc,
        ),
    )(points, centroids)


def solution(mesh):
    def local(points, centroids):
        small = (
            mesh.shape["dp"] == NZ and mesh.shape["cent"] == NC
            and points.shape == (128, 1024) and centroids.shape == (4096, 1024)
        )
        return fused_local(points, centroids) if small else general(points, centroids)

    return jax.shard_map(
        local,
        mesh=mesh,
        in_specs=(P(("dp", "cent"), None), P("cent", None)),
        out_specs=P("dp", "cent"),
        check_vma=False,
    )
```
